512 devices in a mesh: seq: 32 (over z_lo, y), pipe: 4 (over x), dp: 4 (over z_hi, core).
Axes of the slice: x: 4, y: 8, z: 8 (z_hi: 2, z_lo: 4; z = z_hi * 4 + z_lo), core: 2. Of those that a mesh axis runs over, the one named last changes fastest.
Arguments:
- section_inputs: bfloat16 [4, 4, 32, 256, 12, 128], P('pipe', 'dp', 'seq'), may hold values from -6 to 6
- out_grad: bfloat16 [4, 32, 256, 12, 128], P('dp', 'seq'), may hold values from -6 to 6
- gains: float32 [4, 2, 2, 12, 128], P('pipe'), may hold values from -16 to 16
Outputs:
- input_grads: bfloat16 [4, 4, 32, 256, 12, 128], P('pipe', 'dp', 'seq')
- gain_grads: float32 [4, 2, 2, 12, 128], P('pipe')
The draws below stay inside these ranges and needn't reach their ends.
All inputs are finite; a program needn't handle non-finite values.
Results may differ from the reference program's by a relative error of at most 0.035.
Values may be sent and summed in bfloat16 or wider, within the bound.
A program may use at most 64 MiB of HBM per device.

```python
import jax
import jax.numpy as jnp
from jax import lax

HEADS = 12
HD = 128
SPATIAL = 256
FRAMES = 32
BATCH = 4
N_PIPE = 4


def draw_gains(key, part):
    key = jax.random.fold_in(key, 7)
    keys_list = jax.random.split(key, 7)
    shape = (N_PIPE, 2, 2, HEADS, HD)
    base = jnp.clip(jax.random.normal(keys_list[0], shape, jnp.float32), -4.0, 4.0)
    lows = jnp.array([40.0, 45.0], jnp.float32)
    highs = jnp.array([60.0, 70.0], jnp.float32)
    first_head = jax.random.randint(keys_list[1], (N_PIPE, 1), 0, HEADS)
    offset = jax.random.randint(keys_list[2], (N_PIPE, 1), 1, max(HEADS, 2))
    second_head = (first_head + offset) % HEADS
    head_pick = jnp.concatenate([first_head, second_head], axis=1)
    strength = jax.random.uniform(keys_list[4], (N_PIPE, 2), jnp.float32, 0.0, 1.0)
    target = lows[None, :] + strength * (highs - lows)[None, :]
    level = jnp.sqrt(target / HD ** 0.5)
    rough = jax.random.uniform(keys_list[5], (N_PIPE, 2, 2, 1, HD), jnp.float32, 0.9, 1.1)
    signs = (2 * jax.random.randint(keys_list[6], (N_PIPE, 2), 0, 2) - 1).astype(jnp.float32)
    head_ids = lax.broadcasted_iota(jnp.int32, shape, 3)
    chosen = head_ids == head_pick[:, :, None, None, None]
    planted = (signs * level)[:, :, None, None, None] * rough
    return jnp.where(chosen, planted, base).astype(jnp.float32)


def shard_levels(stream_key, extent, shards, smallest, largest):
    factor_of, own = 1.0, jax.random.fold_in(stream_key, 6)
    for position, blocks in shards:
        heights = jnp.exp(jax.random.uniform(jax.random.fold_in(own, position), (blocks,), jnp.float32, smallest / len(shards), largest / len(shards)))
        factor_of = factor_of * jnp.repeat(heights, extent[position] // blocks).reshape([-1 if axis == position else 1 for axis in range(len(extent))])
    return factor_of


def normal_values(key, extent, spread, limit, shards=(), dtype=jnp.bfloat16):
    level = shard_levels(key, extent, shards, -0.22, 0.18) if shards else 1.0
    result = jax.random.normal(key, extent, jnp.float32) * spread * level
    return jnp.minimum(jnp.maximum(result, -limit), limit).astype(dtype)


def setup_inputs(seed: int = 0) -> dict:
    key_list = jax.random.split(jax.random.key(seed), 4)
    section_inputs = normal_values(key_list[0], (N_PIPE, BATCH, FRAMES, SPATIAL, HEADS, HD), 1.0, 6.0, ((0, 4), (1, 4), (2, 32)))
    out_grad = normal_values(key_list[1], (BATCH, FRAMES, SPATIAL, HEADS, HD), 1.0, 6.0, ((0, 4), (1, 32)))
    gains = draw_gains(jax.random.fold_in(key_list[3], 71), 0)
    return dict(section_inputs=section_inputs, out_grad=out_grad, gains=gains)


def normed(values):
    return values * lax.rsqrt(lax.optimization_barrier(jnp.mean(values * values, axis=-1, keepdims=True)) + 1e-06)

def attend(values, gain_q, gain_k, score_form, mix_form):
    rows = normed(values)
    query = (rows * gain_q).astype(jnp.bfloat16)
    keys_part = (rows * gain_k).astype(jnp.bfloat16)
    scores = jnp.einsum(score_form, query, keys_part, preferred_element_type=jnp.float32) * values.shape[-1] ** (-0.5)
    weights = jax.nn.softmax(scores, axis=-1).astype(jnp.bfloat16)
    return jnp.einsum(mix_form, weights, values.astype(jnp.bfloat16), preferred_element_type=jnp.float32)

def spatial_core(values, gain_q, gain_k):
    return attend(values, gain_q, gain_k, 'bfshd,bfthd->bfhst', 'bfhst,bfthd->bfshd')

def temporal_core(values, gain_q, gain_k):
    return attend(values, gain_q, gain_k, 'bfshd,bgshd->bshfg', 'bshfg,bgshd->bfshd')

def section_back(inputs, grad_out, gain):
    inputs_float = inputs.astype(jnp.float32)
    primal, back_space = jax.vjp(spatial_core, inputs_float, gain[0, 0], gain[0, 1])
    mixed = (inputs_float + primal).astype(jnp.bfloat16)
    mixed_float = lax.optimization_barrier(mixed).astype(jnp.float32)
    _, back_time = jax.vjp(temporal_core, mixed_float, gain[1, 0], gain[1, 1])
    time_grad, time_gq, time_gk = back_time(grad_out.astype(jnp.float32))
    resid = (grad_out.astype(jnp.float32) + time_grad).astype(jnp.bfloat16)
    space_grad, space_gq, space_gk = back_space(resid.astype(jnp.float32))
    input_grad = (resid.astype(jnp.float32) + space_grad).astype(jnp.bfloat16)
    step_gains = jnp.stack([jnp.stack([space_gq, space_gk]), jnp.stack([time_gq, time_gk])])
    return (input_grad, step_gains)

def reference(section_inputs, out_grad, gains):
    carried = out_grad
    grads_list = []
    gain_list = []
    for section in reversed(range(N_PIPE)):
        gain = gains[section]
        samples = section_inputs[section][:, None]
        incoming = carried[:, None]

        def one_sample(pair):
            return section_back(pair[0], pair[1], gain)
        input_grad, sample_gains = lax.map(one_sample, (samples, incoming))
        carried = input_grad[:, 0]
        grads_list.append(carried)
        gain_list.append(lax.optimization_barrier(jnp.sum(sample_gains, axis=0)))
    input_grads = jnp.stack(grads_list[::-1])
    gain_grads = jnp.stack(gain_list[::-1])
    return (input_grads, gain_grads)
```

```python
import jax
import jax.numpy as jnp
from jax import lax
from jax.experimental import pallas as pl
from jax.experimental.pallas import tpu as pltpu
from jax.sharding import PartitionSpec as P

MESH = pl.DeviceIdType.MESH
BF = jnp.bfloat16
F32 = jnp.float32
HEADS, HD, TOKENS, FRAMES, SECTIONS = 12, 128, 256, 32, 4
SCALE = HD ** -0.5
EXP2 = SCALE * 1.4426950408889634


def dot(a, b, ca, cb):
    return lax.dot_general(a, b, (((ca,), (cb,)), ((), ())), preferred_element_type=F32)


def attend_fwd(u, gain_q, gain_k, mask):
    r = lax.rsqrt(jnp.mean(u * u, axis=-1, keepdims=True) + 1e-06)
    n = u * r
    q = (n * gain_q).astype(BF)
    k = (n * gain_k).astype(BF)
    st = dot(k, q, 1, 1)
    if mask is not None:
        st = jnp.where(mask, st, -1e30)
    top = jnp.max(st, axis=0, keepdims=True)
    e = jnp.exp2((st - top) * EXP2)
    p = e * (1.0 / jnp.sum(e, axis=0, keepdims=True))
    return r, n, q, k, p


def attend_bwd(do, u, p, pb, q, k, n, r, gain_q, gain_k):
    dp = dot(u, do, 1, 1)
    row = jnp.sum(p * dp, axis=0, keepdims=True)
    ds = (p * (dp - row)).astype(BF)
    du = dot(pb, do, 1, 0)
    dk = dot(ds, q, 1, 0)
    dq = dot(ds, k, 0, 0)
    dn = dq * (gain_q * SCALE) + dk * (gain_k * SCALE)
    along = jnp.mean(dn * n, axis=-1, keepdims=True)
    dx = do.astype(F32) + du + r * (dn - n * along)
    gq = jnp.sum(dq * n, axis=0, keepdims=True) * SCALE
    gk = jnp.sum(dk * n, axis=0, keepdims=True) * SCALE
    return dx, gq, gk


def kernel(a_ref, og_ref, g_ref, out_ref, gout_ref,
           tr, ah, ogh, a_s, og_s, gn, ys, yt, gt, dyt, dys, dxs, outr,
           xf, sp, spb, sq, sk, sn, sr, tx, tp, tpb, tq, tk, tn, trr,
           gsum, ghome, gtot, gbr, gall,
           s_a, r_a, s_og, r_og, s_gn, r_gn, s_y, r_y, s_g, r_g, s_dy, r_dy,
           s_out, r_out, s_p1, r_p1, s_p2, r_p2, s_p3, r_p3):
    seq = lax.axis_index("seq")
    x = lax.axis_index("pipe")
    dp_i = lax.axis_index("dp")
    z_lo, y = seq // 8, seq % 8
    z_hi, c = dp_i // 2, dp_i % 2
    half, yy = y // 4, y % 4
    rest = (yy + 3 - z_lo) % 4
    active = rest < 3
    unit = z_lo + 4 * (3 * half + jnp.minimum(rest, 2))
    u_c, u_h = unit // 12, unit % 12
    d = x * 2 + c

    def dev(xx, y_, zl, zh, cc):
        return {"seq": zl * 8 + y_, "pipe": xx, "dp": zh * 2 + cc}

    def send(src, dst, ssem, rsem, to):
        pltpu.make_async_remote_copy(
            src_ref=src, dst_ref=dst, send_sem=ssem, recv_sem=rsem,
            device_id=to, device_id_type=MESH,
        ).start()

    def copy(src, dst, sem):
        pltpu.make_async_copy(src, dst, sem).start()

    def wait(ref, sem):
        pltpu.make_async_copy(ref, ref, sem).wait()

    def unit_place(cb, h):
        u = cb * 12 + h
        zl, k = u % 4, u // 4
        hf = k // 3
        return hf * 4 + (zl + 1 + k % 3) % 4, zl, hf

    def unit_device(h):
        y_, zl, hf = unit_place(c, h)
        return dev((yy + h) % 4, y_, zl, z_hi, (half + hf + 1 + c) % 2)

    def peer(j):
        p = (d + j) % 8
        return p, dev(p // 2, y, z_lo, z_hi, p % 2)

    def heads_out(src, dst):
        wide = tr.reshape(TOKENS, 16, HD)
        wide[:, 0:HEADS, :] = src[...].astype(F32)
        for h in range(HEADS):
            dst[h] = tr[pl.ds(h, TOKENS, stride=16), :].astype(BF)

    heads_out(a_ref, ah)

    def send_a(h, _):
        send(ah.at[h], a_s.at[x, z_lo], s_a, r_a.at[x], unit_device(h))
        return 0

    lax.fori_loop(0, HEADS, send_a, 0)

    @pl.when(active)
    def _():
        copy(g_ref, gn.at[x], r_gn)

        def send_gain(j, _):
            xx = (x + j) % 4
            send(g_ref, gn.at[x], s_gn, r_gn, dev(xx, y, z_lo, z_hi, c))
            return 0

        lax.fori_loop(1, 4, send_gain, 0)

    heads_out(og_ref, ogh)

    def send_og(m, _):
        h = (x + 4 - yy) % 4 + 4 * m
        send(ogh.at[h], og_s.at[z_lo], s_og, r_og, unit_device(h))
        return 0

    lax.fori_loop(0, 3, send_og, 0)

    gsum[...] = jnp.zeros_like(gsum)

    def to_tokens(src, dst, ssem, rsem):
        copy(src.at[:, pl.ds(pl.multiple_of(d * 32, 32), 32), :], dst.at[d], rsem)

        def one(j, _):
            p, to = peer(j)
            send(src.at[:, pl.ds(pl.multiple_of(p * 32, 32), 32), :], dst.at[d], ssem, rsem, to)
            return 0

        lax.fori_loop(1, 8, one, 0)

    def to_frames(src, dst, ssem, rsem):
        mine = pl.ds(pl.multiple_of(d * 32, 32), 32)
        copy(src.at[d], dst.at[:, mine, :], rsem)

        def one(j, _):
            p, to = peer(j)
            send(src.at[p], dst.at[:, mine, :], ssem, rsem, to)
            return 0

        lax.fori_loop(1, 8, one, 0)

    def gain_row(s, l, j):
        return gn[s, l, j, pl.ds(u_h, 1), :]

    def spatial_fwd(s):
        gq, gk = gain_row(s, 0, 0), gain_row(s, 0, 1)

        def one(i, _):
            ab = a_s[s, i]
            u = ab.astype(F32)
            r, n, q, k, p = attend_fwd(u, gq, gk, None)
            pb = p.astype(BF)
            sp[i] = p
            spb[i] = pb
            sq[i] = q
            sk[i] = k
            sn[i] = n
            sr[i] = jnp.broadcast_to(r, n.shape)
            ys[s, i] = (u + dot(pb, ab, 0, 0)).astype(BF)
            return 0

        lax.fori_loop(0, 4, one, 0, unroll=2)

    def spatial_bwd(s):
        gq, gk = gain_row(s, 0, 0), gain_row(s, 0, 1)

        def one(i, total):
            dx, dgq, dgk = attend_bwd(
                dys[s, i], a_s[s, i], sp[i], spb[i], sq[i], sk[i], sn[i], sr[i], gq, gk)
            dxs[s, i] = dx.astype(BF)
            return total[0] + dgq, total[1] + dgk

        zero = jnp.zeros((1, HD), F32)
        dgq, dgk = lax.fori_loop(0, 4, one, (zero, zero), unroll=2)
        gsum[s, 0:1, :] = dgq
        gsum[s, 1:2, :] = dgk

    ri = lax.broadcasted_iota(jnp.int32, (128, 128), 0)
    ci = lax.broadcasted_iota(jnp.int32, (128, 128), 1)
    same = (ri // 32) == (ci // 32)

    def by_token(src):
        xf[...] = src[...].reshape(FRAMES * 32, HD).astype(F32)

    def token_rows(b):
        return jnp.concatenate(
            [xf[pl.ds(b * 4 + t, FRAMES, stride=32), :] for t in range(4)], axis=0)

    def temporal_fwd(s):
        by_token(yt.at[s])
        gq, gk = gain_row(s, 1, 0), gain_row(s, 1, 1)

        def one(b, _):
            u = token_rows(b)
            r, n, q, k, p = attend_fwd(u, gq, gk, same)
            tx[b] = u.astype(BF)
            tp[b] = p
            tpb[b] = p.astype(BF)
            tq[b] = q
            tk[b] = k
            tn[b] = n
            trr[b] = jnp.broadcast_to(r, n.shape)
            return 0

        lax.fori_loop(0, 8, one, 0, unroll=4)

    def temporal_bwd(s):
        by_token(gt.at[s])
        gq, gk = gain_row(s, 1, 0), gain_row(s, 1, 1)

        def one(b, total):
            do = token_rows(b).astype(BF)
            dx, dgq, dgk = attend_bwd(
                do, tx[b], tp[b], tpb[b], tq[b], tk[b], tn[b], trr[b], gq, gk)
            for t in range(4):
                xf[pl.ds(b * 4 + t, FRAMES, stride=32), :] = dx[t * 32:(t + 1) * 32]
            return total[0] + dgq, total[1] + dgk

        zero = jnp.zeros((1, HD), F32)
        dgq, dgk = lax.fori_loop(0, 8, one, (zero, zero), unroll=4)
        dyt[s] = xf[...].astype(BF).reshape(8, 4, 32, HD)
        gsum[s, 2:3, :] = dgq
        gsum[s, 3:4, :] = dgk

    @pl.when(active)
    def _():
        wait(gn, r_gn)
        last = SECTIONS - 1
        wait(a_s.at[last], r_a.at[last])
        spatial_fwd(last)
        to_tokens(ys.at[last], yt.at[last], s_y.at[last], r_y.at[last])
        wait(og_s, r_og)
        to_tokens(og_s, gt.at[last], s_g.at[last], r_g.at[last])
        wait(yt.at[last], r_y.at[last])
        temporal_fwd(last)

        def section(step, _):
            s = last - step
            before = jnp.maximum(s - 1, 0)
            wait(gt.at[s], r_g.at[s])
            temporal_bwd(s)
            to_frames(dyt.at[s], dys.at[s], s_dy.at[s], r_dy.at[s])
            wait(dys.at[s], r_dy.at[s])
            spatial_bwd(s)

            @pl.when(s > 0)
            def _():
                to_tokens(dxs.at[s], gt.at[before], s_g.at[before], r_g.at[before])

            def send_out(i, _):
                h = u_h
                y4 = (x + 12 - h) % 4
                y_f = y4 + 4 * ((c + half + 1 + u_c) % 2)
                send(dxs.at[s, i], outr.at[h], s_out.at[s], r_out, dev(s, y_f, i, z_hi, u_c))
                return 0

            lax.fori_loop(0, 4, send_out, 0)

            @pl.when(s > 0)
            def _():
                wait(a_s.at[before], r_a.at[before])
                spatial_fwd(before)
                to_tokens(ys.at[before], yt.at[before], s_y.at[before], r_y.at[before])
                wait(yt.at[before], r_y.at[before])
                temporal_fwd(before)

            return 0

        lax.fori_loop(0, SECTIONS, section, 0)

        home = u_h // 2

        def send_home(s, _):
            to = dev(s, home, home % 4, home // 4, u_h % 2)
            at = ghome.at[z_hi, u_c, x, c]
            me_home = ((x == s) & (y == home) & (z_lo == home % 4)
                       & (z_hi == home // 4) & (c == u_h % 2))

            @pl.when(me_home)
            def _():
                copy(gsum.at[s], at, r_p1)

            @pl.when(jnp.logical_not(me_home))
            def _():
                send(gsum.at[s], at, s_p1.at[s], r_p1, to)
                wait(gsum.at[s], s_p1.at[s])

            return 0

        lax.fori_loop(0, SECTIONS, send_home, 0)

    z = z_hi * 4 + z_lo
    is_home = (y < 6) & (z == y)

    @pl.when(is_home)
    def _():
        wait(ghome, r_p1)
        gtot[...] = jnp.sum(ghome[...].reshape(32, 8, HD), axis=0)
        copy(gtot, gbr.at[c], r_p2)

        def spread(j, _):
            e = (z * 2 + c + j) % 16
            ez = e // 2
            send(gtot, gbr.at[c], s_p2.at[j], r_p2, dev(x, y, ez % 4, ez // 4, e % 2))
            return 0

        lax.fori_loop(1, 16, spread, 0)

    @pl.when(y < 6)
    def _():
        wait(gbr, r_p2)
        copy(gbr, gall.at[y], r_p3)

        def along(j, _):
            send(gbr, gall.at[y], s_p3.at[j], r_p3, dev(x, (y + j) % 8, z_lo, z_hi, c))
            return 0

        lax.fori_loop(1, 8, along, 0)

    wait(outr, r_out)
    for h in range(HEADS):
        tr[pl.ds(h, TOKENS, stride=16), :] = outr[h].astype(F32)
    out_ref[...] = tr.reshape(TOKENS, 16, HD)[:, 0:HEADS, :].astype(BF)

    wait(gall, r_p3)
    for h in range(HEADS):
        for l in range(2):
            for j in range(2):
                gout_ref[l, j, h:h + 1, :] = gall[h // 2, h % 2, 2 * l + j:2 * l + j + 1, :]

    wait(ah, s_a)
    wait(ogh.at[pl.ds(0, 3)], s_og)

    @pl.when(active)
    def _():
        wait(gn.at[pl.ds(0, 3)], s_gn)

        def drain(s, _):
            wait(dyt.at[s, pl.ds(0, 7)], s_y.at[s])
            wait(dyt.at[s, pl.ds(0, 7)], s_g.at[s])
            wait(dyt.at[s, pl.ds(0, 7)], s_dy.at[s])
            wait(dxs.at[s], s_out.at[s])
            return 0

        lax.fori_loop(0, SECTIONS, drain, 0)

    @pl.when(is_home)
    def _():
        def drain(j, _):
            wait(gtot, s_p2.at[j])
            return 0

        lax.fori_loop(1, 16, drain, 0)

    @pl.when(y < 6)
    def _():
        def drain(j, _):
            wait(gbr, s_p3.at[j])
            return 0

        lax.fori_loop(1, 8, drain, 0)


def per_device(section_inputs, out_grad, gains):
    a = section_inputs.reshape(TOKENS, HEADS, HD)
    og = out_grad.reshape(TOKENS, HEADS, HD)
    g = gains.reshape(2, 2, HEADS, HD)
    V, D = pltpu.VMEM, pltpu.SemaphoreType.DMA
    s4 = (SECTIONS,)
    scratch = [
        V((TOKENS * 16, HD), F32),
        V((HEADS, TOKENS, HD), BF),
        V((HEADS, TOKENS, HD), BF),
        V((4, 4, TOKENS, HD), BF),
        V((4, TOKENS, HD), BF),
        V((4, 2, 2, HEADS, HD), F32),
        V((4, 4, TOKENS, HD), BF),
        V((4, 8, 4, 32, HD), BF),
        V((4, 8, 4, 32, HD), BF),
        V((4, 8, 4, 32, HD), BF),
        V((4, 4, TOKENS, HD), BF),
        V((4, 4, TOKENS, HD), BF),
        V((HEADS, TOKENS, HD), BF),
        V((FRAMES * 32, HD), F32),
        V((4, TOKENS, TOKENS), F32),
        V((4, TOKENS, TOKENS), BF),
        V((4, TOKENS, HD), BF),
        V((4, TOKENS, HD), BF),
        V((4, TOKENS, HD), F32),
        V((4, TOKENS, HD), F32),
        V((8, 128, HD), BF),
        V((8, 128, 128), F32),
        V((8, 128, 128), BF),
        V((8, 128, HD), BF),
        V((8, 128, HD), BF),
        V((8, 128, HD), F32),
        V((8, 128, HD), F32),
        V((4, 8, HD), F32),
        V((2, 2, 4, 2, 8, HD), F32),
        V((8, HD), F32),
        V((2, 8, HD), F32),
        V((6, 2, 8, HD), F32),
        D, D(s4), D, D, D, D, D(s4), D(s4), D(s4), D(s4), D(s4), D(s4),
        D(s4), D, D(s4), D, D((16,)), D, D((8,)), D,
    ]
    vm = pl.BlockSpec(memory_space=pltpu.VMEM)
    grads, gain_grads = pl.pallas_call(
        kernel,
        out_shape=(
            jax.ShapeDtypeStruct((TOKENS, HEADS, HD), BF),
            jax.ShapeDtypeStruct((2, 2, HEADS, HD), F32),
        ),
        in_specs=[vm, vm, vm],
        out_specs=(vm, vm),
        scratch_shapes=scratch,
        compiler_params=pltpu.CompilerParams(
            has_side_effects=True, vmem_limit_bytes=48 * 1024 * 1024),
        name="sections_back",
    )(a, og, g)
    return grads.reshape(section_inputs.shape), gain_grads[None]


def solution(mesh):
    return jax.shard_map(
        per_device,
        mesh=mesh,
        in_specs=(
            P("pipe", "dp", "seq", None, None, None),
            P("dp", "seq", None, None, None),
            P("pipe", None, None, None, None),
        ),
        out_specs=(P("pipe", "dp", "seq", None, None, None), P("pipe", None, None, None, None)),
        check_vma=False,
    )
```

```python
import jax
import jax.numpy as jnp
from jax import lax
from jax.experimental import pallas as pl
from jax.experimental.pallas import tpu as pltpu
from jax.sharding import PartitionSpec as P

MESH = pl.DeviceIdType.MESH
BF = jnp.bfloat16
F32 = jnp.float32
HEADS, HD, TOKENS, FRAMES, SECTIONS = 12, 128, 256, 32, 4
SCALE = HD ** -0.5
EXP2 = SCALE * 1.4426950408889634


def dot(a, b, ca, cb):
    return lax.dot_general(a, b, (((ca,), (cb,)), ((), ())), preferred_element_type=F32)


def attend_fwd(u, gain_q, gain_k, mask):
    r = lax.rsqrt(jnp.mean(u * u, axis=-1, keepdims=True) + 1e-06)
    n = u * r
    q = (n * gain_q).astype(BF)
    k = (n * gain_k).astype(BF)
    st = dot(k, q, 1, 1)
    if mask is not None:
        st = jnp.where(mask, st, -1e30)
    top = jnp.max(st, axis=0, keepdims=True)
    e = jnp.exp2((st - top) * EXP2)
    p = e * (1.0 / jnp.sum(e, axis=0, keepdims=True))
    return r, n, q, k, p


def attend_bwd(do, u, p, pb, q, k, n, r, gain_q, gain_k):
    dp = dot(u, do, 1, 1)
    row = jnp.sum(p * dp, axis=0, keepdims=True)
    ds = (p * (dp - row)).astype(BF)
    du = dot(pb, do, 1, 0)
    dk = dot(ds, q, 1, 0)
    dq = dot(ds, k, 0, 0)
    dn = dq * (gain_q * SCALE) + dk * (gain_k * SCALE)
    along = jnp.mean(dn * n, axis=-1, keepdims=True)
    dx = do.astype(F32) + du + r * (dn - n * along)
    gq = jnp.sum(dq * n, axis=0, keepdims=True) * SCALE
    gk = jnp.sum(dk * n, axis=0, keepdims=True) * SCALE
    return dx, gq, gk


def kernel(a_ref, og_ref, g_ref, out_ref, gout_ref,
           l1a, a_s, og_s, gn, ys, yt, gt, dyt, dys, dxs, l1o,
           xf, xo, sp, spb, sq, sk, sn, sr, tx, tp, tpb, tq, tk, tn, trr,
           gsum, gcol, gunit, gl1, gall, gother,
           s_a1, r_a1, s_a2, r_a2, s_og, r_og, s_gn, r_gn, s_y, r_y, s_g, r_g, s_dy, r_dy,
           s_o1, r_o1, s_o2, r_o2, s_p1, r_p1, s_p2, r_p2, s_p3, r_p3, s_p4, r_p4, go):
    seq = lax.axis_index("seq")
    x = lax.axis_index("pipe")
    dp_i = lax.axis_index("dp")
    z_lo, y = seq // 8, seq % 8
    z_hi, c = dp_i // 2, dp_i % 2
    half, yy = y // 4, y % 4
    rest = (yy + 3 - z_lo) % 4
    active = rest < 3
    u_c = half
    u_m = jnp.minimum(rest, 2)
    u_r = (z_lo + 4 - u_m) % 4
    u_h = u_r + 4 * u_m
    d = x * 2 + c
    last = SECTIONS - 1

    def dev(xx, y_, zl, zh, cc):
        return {"seq": zl * 8 + y_, "pipe": xx, "dp": zh * 2 + cc}

    def send(src, dst, ssem, rsem, to):
        pltpu.make_async_remote_copy(
            src_ref=src, dst_ref=dst, send_sem=ssem, recv_sem=rsem,
            device_id=to, device_id_type=MESH,
        ).start()

    def copy(src, dst, sem):
        pltpu.make_async_copy(src, dst, sem).start()

    def wait(ref, sem):
        pltpu.make_async_copy(ref, ref, sem).wait()

    def loop(lo, hi, body):
        def step(i, _):
            body(i)
            return 0

        lax.fori_loop(lo, hi, step, 0)

    def head_row(plane):
        return (plane + 4 - yy + z_lo) % 4

    def unit_device(m):
        zl = (head_row(x) + m) % 4
        return dev(x, 4 * c + (zl + 1 + m) % 4, zl, z_hi, (half + 1) % 2)

    def frame_device(i):
        return dev(x, (x + i + 4 - u_r) % 4 + 4 * ((c + 1) % 2), i, z_hi, u_c)

    def peers():
        for dx in (2, 1, 3, 0):
            for cc in (c, 1 - c) if dx else (1 - c,):
                xx = (x + dx) % 4
                yield xx * 2 + cc, dev(xx, y, z_lo, z_hi, cc)

    def along_x(j):
        xx = (x + j) % 4
        return xx, dev(xx, y, z_lo, z_hi, c)

    samples = [dev(x, y, z_lo, 1 - z_hi, c), dev(x, y, z_lo, 1 - z_hi, 1 - c),
               dev(x, y, z_lo, z_hi, 1 - c)]

    barrier = pltpu.get_barrier_semaphore()

    def greet(to):
        pl.semaphore_signal(barrier, inc=1, device_id=to, device_id_type=MESH)

    for _, to in peers():
        greet(to)
    loop(0, 3, lambda m: greet(unit_device(m)))
    greet(samples[0])
    greet(samples[1])

    @pl.when(active)
    def _():
        loop(0, 4, lambda i: greet(frame_device(i)))
        pl.semaphore_wait(barrier, 16)

    @pl.when(jnp.logical_not(active))
    def _():
        pl.semaphore_wait(barrier, 12)

    def hop_a(m):
        copy(a_ref.at[m, head_row(x)], l1a.at[x, m], r_a1.at[x, m])

        def one(j):
            xx, to = along_x(j)
            send(a_ref.at[m, head_row(xx)], l1a.at[x, m], s_a1, r_a1.at[x, m], to)

        loop(1, 4, one)

    loop(0, 3, lambda j: hop_a((j + z_lo) % 3))
    copy(g_ref, gn.at[x], r_gn)
    loop(1, 4, lambda j: send(g_ref, gn.at[x], s_gn, r_gn, along_x(j)[1]))
    def send_og(j):
        m = (j + z_lo) % 3
        send(og_ref.at[m, head_row(x)], og_s.at[z_lo], s_og, r_og, unit_device(m))

    loop(0, 3, send_og)
    gsum[...] = jnp.zeros_like(gsum)

    def forward_a(s):
        def one(j):
            m = (j + z_lo) % 3
            wait(l1a.at[s, m], r_a1.at[s, m])
            send(l1a.at[s, m], a_s.at[s, z_lo], s_a2.at[s], r_a2.at[s], unit_device(m))

        loop(0, 3, one)

    def hop_out(s):
        row = head_row(x)

        @pl.when(x == s)
        def _():
            def one(m):
                wait(l1o.at[s, m], r_o1.at[s, m])
                copy(l1o.at[s, m], out_ref.at[m, row], r_o2)

            loop(0, 3, one)

        @pl.when(x != s)
        def _():
            def one(m):
                wait(l1o.at[s, m], r_o1.at[s, m])
                send(l1o.at[s, m], out_ref.at[m, row], s_o2.at[s], r_o2, dev(s, y, z_lo, z_hi, c))

            loop(0, 3, one)

    def hop_gains(s):
        row = head_row(x)
        wait(gl1.at[s], r_p2.at[s])

        @pl.when(x == s)
        def _():
            copy(gl1.at[s], gall.at[row], r_p3)

        @pl.when(x != s)
        def _():
            send(gl1.at[s], gall.at[row], s_p3.at[s], r_p3, dev(s, y, z_lo, z_hi, c))

    def share_gains(s):
        copy(gsum.at[s], gcol.at[s, d], r_p1.at[s])
        for _, to in peers():
            send(gsum.at[s], gcol.at[s, d], s_p1.at[s], r_p1.at[s], to)

    def unit_gains(s):
        wait(gcol.at[s], r_p1.at[s])
        gunit[s] = jnp.sum(gcol[s], axis=0)
        loop(0, 4, lambda i: send(
            gunit.at[s], gl1.at[s, u_m], s_p2.at[s], r_p2.at[s], frame_device(i)))

    def send_out(s, lo, hi):
        loop(lo, hi, lambda i: send(
            dxs.at[s, i], l1o.at[s, u_m], s_o1.at[s], r_o1.at[s, u_m],
            frame_device(i)))

    def to_tokens(src, dst, ssem, rsem, first=0, frames=4):
        fr = pl.ds(first, frames)

        def rows(p):
            return src.at[fr, pl.ds(pl.multiple_of(p * 32, 32), 32), :]

        copy(rows(d), dst.at[d, fr], rsem)

        for p, to in peers():
            send(rows(p), dst.at[d, fr], ssem, rsem, to)

    def to_frames(src, dst, ssem, rsem, first):
        mine = pl.ds(pl.multiple_of(d * 32 + first, 16), 16)
        part = pl.ds(first, 16)
        copy(src.at[d, :, part, :], dst.at[:, mine, :], rsem)

        for p, to in peers():
            send(src.at[p, :, part, :], dst.at[:, mine, :], ssem, rsem, to)

    def gain_row(s, l, j):
        return gn[s, l, u_h, j:j + 1, :]

    def spatial_fwd(s):
        gq, gk = gain_row(s, 0, 0), gain_row(s, 0, 1)
        b = s % 2

        def one(i, _):
            ab = a_s[s, i]
            u = ab.astype(F32)
            r, n, q, k, p = attend_fwd(u, gq, gk, None)
            pb = p.astype(BF)
            sp[b, i] = p
            spb[b, i] = pb
            sq[b, i] = q
            sk[b, i] = k
            sn[b, i] = n
            sr[b, i] = jnp.broadcast_to(r, n.shape)
            ys[s, i] = (u + dot(pb, ab, 0, 0)).astype(BF)
            return 0

        lax.fori_loop(0, 4, one, 0, unroll=2)

    def add_gains(s, l, dgq, dgk):
        gsum[s, 2 * l:2 * l + 1, :] += dgq
        gsum[s, 2 * l + 1:2 * l + 2, :] += dgk

    def spatial_bwd(s, first):
        gq, gk = gain_row(s, 0, 0), gain_row(s, 0, 1)
        b = s % 2
        for i in (first, first + 1):
            dx, dgq, dgk = attend_bwd(
                dys[s, i], a_s[s, i], sp[b, i], spb[b, i], sq[b, i], sk[b, i], sn[b, i],
                sr[b, i], gq, gk)
            dxs[s, i] = dx.astype(BF)
            add_gains(s, 0, dgq, dgk)

    ri = lax.broadcasted_iota(jnp.int32, (128, 128), 0)
    ci = lax.broadcasted_iota(jnp.int32, (128, 128), 1)
    same = (ri // 32) == (ci // 32)

    def by_token(src):
        xf[...] = src[...].reshape(FRAMES * 32, HD).astype(F32)

    def token_rows(b):
        return jnp.concatenate(
            [xf[pl.ds(b * 4 + t, FRAMES, stride=32), :] for t in range(4)], axis=0)

    def temporal_fwd(s):
        by_token(yt.at[s])
        gq, gk = gain_row(s, 1, 0), gain_row(s, 1, 1)
        for b in range(8):
            u = token_rows(b)
            r, n, q, k, p = attend_fwd(u, gq, gk, same)
            tx[b] = u.astype(BF)
            tp[b] = p
            tpb[b] = p.astype(BF)
            tq[b] = q
            tk[b] = k
            tn[b] = n
            trr[b] = jnp.broadcast_to(r, n.shape)

    def temporal_bwd(s, first):
        gq, gk = gain_row(s, 1, 0), gain_row(s, 1, 1)
        for b in range(first, first + 4):
            dx, dgq, dgk = attend_bwd(
                token_rows(b).astype(BF), tx[b], tp[b], tpb[b], tq[b], tk[b], tn[b], trr[b],
                gq, gk)
            for t in range(4):
                xo[pl.ds(b * 4 + t, FRAMES, stride=32), :] = dx[t * 32:(t + 1) * 32]
            add_gains(s, 1, dgq, dgk)
        part = slice(4 * first, 4 * first + 16)
        dyt[s, :, :, part, :] = xo.reshape(8, 4, 32, HD)[:, :, part, :].astype(BF)

    forward_a(last)

    @pl.when(active)
    def _():
        wait(og_s, r_og)
        to_tokens(og_s, gt.at[last], s_g.at[last], r_g.at[last])
        wait(gn, r_gn)
        wait(a_s.at[last], r_a2.at[last])
        spatial_fwd(last)
        to_tokens(ys.at[last], yt.at[last], s_y.at[last], r_y.at[last])
        loop(0, 4, lambda i: pl.semaphore_signal(
            go, inc=1, device_id=frame_device(i), device_id_type=MESH))
        forward_a(last - 1)
        wait(yt.at[last], r_y.at[last])
        temporal_fwd(last)

        def section(step):
            s = last - step
            before = jnp.maximum(s - 1, 0)
            after = jnp.minimum(s + 1, last)
            wait(gt.at[s], r_g.at[s])
            by_token(gt.at[s])
            for part in range(2):
                temporal_bwd(s, 4 * part)
                to_frames(dyt.at[s], dys.at[s], s_dy.at[s], r_dy.at[s], 16 * part)

            @pl.when(s == last)
            def _():
                forward_a(1)
                forward_a(0)

            @pl.when(s > 0)
            def _():
                wait(a_s.at[before], r_a2.at[before])
                spatial_fwd(before)
                to_tokens(ys.at[before], yt.at[before], s_y.at[before], r_y.at[before])

            @pl.when(s < last)
            def _():
                unit_gains(after)

            wait(dys.at[s], r_dy.at[s])

            @pl.when(s == 0)
            def _():
                hop_out(3)

            for part in range(2):
                spatial_bwd(s, 2 * part)

                @pl.when(s > 0)
                def _():
                    to_tokens(dxs.at[s], gt.at[before], s_g.at[before], r_g.at[before],
                              2 * part, 2)

                @pl.when(s == 0)
                def _():
                    send_out(s, 2 * part, 2 * part + 2)

            @pl.when(s > 0)
            def _():
                wait(yt.at[before], r_y.at[before])
                temporal_fwd(before)
                send_out(s, 0, 4)

            share_gains(s)

        loop(0, SECTIONS, section)
        hop_out(2)
        hop_out(1)
        pl.semaphore_wait(go, 3)
        loop(0, SECTIONS - 1, lambda j: hop_gains(last - j))
        unit_gains(0)

    @pl.when(jnp.logical_not(active))
    def _():
        wait(gn, r_gn)
        pl.semaphore_wait(go, 3)
        loop(1, SECTIONS, lambda j: forward_a(last - j))

        def relay(j):
            hop_out(last - j)
            hop_gains(last - j)

        loop(0, SECTIONS - 1, relay)

    hop_out(0)
    hop_gains(0)

    wait(gall, r_p3)
    for j, to in enumerate(samples):
        send(gall, gother.at[j], s_p4, r_p4, to)
    wait(gother, r_p4)
    for row in range(4):
        for m in range(3):
            total = gall[row, m] + (gother[0, row, m] + gother[1, row, m] + gother[2, row, m])
            for l in range(2):
                gout_ref[l, row + 4 * m] = total[2 * l:2 * l + 2]

    wait(out_ref, r_o2)

    wait(l1a.at[pl.ds(0, 3)], s_a1)
    wait(og_s.at[pl.ds(0, 3)], s_og)
    wait(gn.at[pl.ds(0, 3)], s_gn)
    wait(gother, s_p4)

    def drain(s):
        wait(l1a.at[s], s_a2.at[s])

        @pl.when(x != s)
        def _():
            wait(l1o.at[s], s_o2.at[s])
            wait(gl1.at[s], s_p3.at[s])

    loop(0, SECTIONS, drain)

    @pl.when(active)
    def _():
        def drain(s):
            wait(dyt.at[s, pl.ds(0, 7)], s_y.at[s])
            wait(dyt.at[s, pl.ds(0, 7)], s_g.at[s])
            wait(dyt.at[s, pl.ds(0, 7)], s_dy.at[s])
            wait(dxs.at[s], s_o1.at[s])
            wait(gcol.at[s, pl.ds(0, 7)], s_p1.at[s])
            wait(gcol.at[s, pl.ds(0, 4)], s_p2.at[s])

        loop(0, SECTIONS, drain)


def per_device(section_inputs, out_grad, gains):
    def by_head(block):
        return block.reshape(TOKENS, HEADS, HD).transpose(1, 0, 2).reshape(3, 4, TOKENS, HD)

    a, og = by_head(section_inputs), by_head(out_grad)
    g = gains.reshape(2, 2, HEADS, HD).transpose(0, 2, 1, 3)
    V, D = pltpu.VMEM, pltpu.SemaphoreType.DMA
    s4, s43 = (SECTIONS,), (SECTIONS, 3)
    scratch = [
        V((4, 3, TOKENS, HD), BF),
        V((4, 4, TOKENS, HD), BF),
        V((4, TOKENS, HD), BF),
        V((4, 2, HEADS, 2, HD), F32),
        V((4, 4, TOKENS, HD), BF),
        V((4, 8, 4, 32, HD), BF),
        V((4, 8, 4, 32, HD), BF),
        V((4, 8, 4, 32, HD), BF),
        V((4, 4, TOKENS, HD), BF),
        V((4, 4, TOKENS, HD), BF),
        V((4, 3, TOKENS, HD), BF),
        V((FRAMES * 32, HD), F32),
        V((FRAMES * 32, HD), F32),
        V((2, 4, TOKENS, TOKENS), F32),
        V((2, 4, TOKENS, TOKENS), BF),
        V((2, 4, TOKENS, HD), BF),
        V((2, 4, TOKENS, HD), BF),
        V((2, 4, TOKENS, HD), F32),
        V((2, 4, TOKENS, HD), F32),
        V((8, 128, HD), BF),
        V((8, 128, 128), F32),
        V((8, 128, 128), BF),
        V((8, 128, HD), BF),
        V((8, 128, HD), BF),
        V((8, 128, HD), F32),
        V((8, 128, HD), F32),
        V((4, 4, HD), F32),
        V((4, 8, 4, HD), F32),
        V((4, 4, HD), F32),
        V((4, 3, 4, HD), F32),
        V((4, 3, 4, HD), F32),
        V((3, 4, 3, 4, HD), F32),
        D, D(s43), D(s4), D(s4), D, D, D, D, D(s4), D(s4), D(s4), D(s4), D(s4), D(s4),
        D(s4), D(s43), D(s4), D, D(s4), D(s4), D(s4), D(s4), D(s4), D, D, D, pltpu.SemaphoreType.REGULAR,
    ]
    vm = pl.BlockSpec(memory_space=pltpu.VMEM)
    hbm = pl.BlockSpec(memory_space=pltpu.HBM)
    grads, gain_grads = pl.pallas_call(
        kernel,
        out_shape=(
            jax.ShapeDtypeStruct((3, 4, TOKENS, HD), BF),
            jax.ShapeDtypeStruct((2, HEADS, 2, HD), F32),
        ),
        in_specs=[hbm, hbm, hbm],
        out_specs=(vm, vm),
        scratch_shapes=scratch,
        compiler_params=pltpu.CompilerParams(
            has_side_effects=True, collective_id=0, vmem_limit_bytes=40 * 1024 * 1024),
        name="sections_back",
    )(a, og, g)
    grads = grads.reshape(HEADS, TOKENS, HD).transpose(1, 0, 2).reshape(section_inputs.shape)
    return grads, gain_grads.transpose(0, 2, 1, 3)[None]


def solution(mesh):
    return jax.shard_map(
        per_device,
        mesh=mesh,
        in_specs=(
            P("pipe", "dp", "seq", None, None, None),
            P("dp", "seq", None, None, None),
            P("pipe", None, None, None, None),
        ),
        out_specs=(P("pipe", "dp", "seq", None, None, None), P("pipe", None, None, None, None)),
        check_vma=False,
    )
```

```python
import jax
import jax.numpy as jnp
from jax import lax
from jax.experimental import pallas as pl
from jax.experimental.pallas import tpu as pltpu
from jax.sharding import PartitionSpec as P

MESH = pl.DeviceIdType.MESH
BF = jnp.bfloat16
F32 = jnp.float32
HEADS, HD, TOKENS, FRAMES, SECTIONS = 12, 128, 256, 32, 4
SCALE = HD ** -0.5
EXP2 = SCALE * 1.4426950408889634


def dot(a, b, ca, cb):
    return lax.dot_general(a, b, (((ca,), (cb,)), ((), ())), preferred_element_type=F32)


def attend_fwd(us, gain_q, gain_k, mask):
    rs = [lax.rsqrt(jnp.mean(u * u, axis=-1, keepdims=True) + 1e-06) for u in us]
    ns = [u * r for u, r in zip(us, rs)]
    qs = [(n * gain_q).astype(BF) for n in ns]
    ks = [(n * gain_k).astype(BF) for n in ns]
    ps = []
    for st in [dot(k, q, 1, 1) for k, q in zip(ks, qs)]:
        if mask is not None:
            st = jnp.where(mask, st, -1e30)
        top = jnp.max(st, axis=0, keepdims=True)
        e = jnp.exp2((st - top) * EXP2)
        ps.append(e * (1.0 / jnp.sum(e, axis=0, keepdims=True)))
    return rs, ns, qs, ks, ps


def attend_bwd(blocks, gain_q, gain_k):
    dps = [dot(u, do, 1, 1) for do, u, p, pb, q, k, n, r in blocks]
    dus = [dot(pb, do, 1, 0) for do, u, p, pb, q, k, n, r in blocks]
    dss = []
    for dp, (do, u, p, pb, q, k, n, r) in zip(dps, blocks):
        row = jnp.sum(p * dp, axis=0, keepdims=True)
        dss.append((p * (dp - row)).astype(BF))
    dks = [dot(ds, b[4], 1, 0) for ds, b in zip(dss, blocks)]
    dqs = [dot(ds, b[5], 0, 0) for ds, b in zip(dss, blocks)]
    dxs, gq, gk = [], 0.0, 0.0
    for dk, dq, du, (do, u, p, pb, q, k, n, r) in zip(dks, dqs, dus, blocks):
        dn = dq * (gain_q * SCALE) + dk * (gain_k * SCALE)
        along = jnp.mean(dn * n, axis=-1, keepdims=True)
        dxs.append(do.astype(F32) + du + r * (dn - n * along))
        gq = gq + jnp.sum(dq * n, axis=0, keepdims=True)
        gk = gk + jnp.sum(dk * n, axis=0, keepdims=True)
    return dxs, gq * SCALE, gk * SCALE


def kernel(a_ref, og_ref, g_ref, out_ref, gout_ref,
           l1a, a_s, og_s, gn, ys, yt, gt, dyt, dys, dxs, l1o,
           xf, xo, sp, spb, sq, sk, sn, sr, tx, tp, tpb, tq, tk, tn, trr,
           gsum, gcol, gunit, gl1, ghop, gall,
           s_a1, r_a1, s_a2, r_a2, s_og, r_og, s_gn, r_gn, s_y, r_y, s_g, r_g, s_dy, r_dy,
           s_o1, r_o1, s_o2, r_o2, s_p1, r_p1, s_p2, r_p2, s_p3, r_p3, go):
    seq = lax.axis_index("seq")
    x = lax.axis_index("pipe")
    dp_i = lax.axis_index("dp")
    z_lo, y = seq // 8, seq % 8
    z_hi, c = dp_i // 2, dp_i % 2
    half, yy = y // 4, y % 4
    rest = (yy + 3 - z_lo) % 4
    active = rest < 3
    u_c = half
    u_m = jnp.minimum(rest, 2)
    u_r = (z_lo + 4 - u_m) % 4
    u_h = u_r + 4 * u_m
    d = x * 2 + c
    last = SECTIONS - 1

    def dev(xx, y_, zl, zh, cc):
        return {"seq": zl * 8 + y_, "pipe": xx, "dp": zh * 2 + cc}

    def send(src, dst, ssem, rsem, to):
        pltpu.make_async_remote_copy(
            src_ref=src, dst_ref=dst, send_sem=ssem, recv_sem=rsem,
            device_id=to, device_id_type=MESH,
        ).start()

    def copy(src, dst, sem):
        pltpu.make_async_copy(src, dst, sem).start()

    def wait(ref, sem):
        pltpu.make_async_copy(ref, ref, sem).wait()

    def loop(lo, hi, body):
        def step(i, _):
            body(i)
            return 0

        lax.fori_loop(lo, hi, step, 0)

    def head_row(plane):
        return (plane + 4 - yy + z_lo) % 4

    def unit_device(m):
        zl = (head_row(x) + m) % 4
        return dev(x, 4 * c + (zl + 1 + m) % 4, zl, z_hi, (half + 1) % 2)

    def frame_device(i):
        return dev(x, (x + i + 4 - u_r) % 4 + 4 * ((c + 1) % 2), i, z_hi, u_c)

    def peers():
        for dx in (2, 1, 3, 0):
            for cc in (c, 1 - c) if dx else (1 - c,):
                xx = (x + dx) % 4
                yield xx * 2 + cc, dev(xx, y, z_lo, z_hi, cc)

    def along_x(j):
        xx = (x + j) % 4
        return xx, dev(xx, y, z_lo, z_hi, c)

    def sample_units(m):
        zl = (head_row(x) + m) % 4
        for zh in range(2):
            for cc in range(2):
                yield dev(x, 4 * cc + (zl + 1 + m) % 4, zl, zh, (half + 1) % 2)

    def sample_frames(i):
        y_f = (x + i + 4 - u_r) % 4 + 4 * ((c + 1) % 2)
        for zh in range(2):
            for cc in range(2):
                yield dev(x, y_f, i, zh, cc)

    barrier = pltpu.get_barrier_semaphore()

    def greet(to):
        pl.semaphore_signal(barrier, inc=1, device_id=to, device_id_type=MESH)

    for _, to in peers():
        greet(to)

    def is_me(to):
        return (to["seq"] == seq) & (to["dp"] == dp_i)

    own = active & ((x + z_lo + 4 - u_r) % 4 + 4 * ((c + 1) % 2) == y)

    def greet_all(devices):
        for to in devices:
            @pl.when(jnp.logical_not(is_me(to)))
            def _():
                greet(to)

    loop(0, 3, lambda m: greet_all(sample_units(m)))

    @pl.when(active)
    def _():
        loop(0, 4, lambda i: greet_all(sample_frames(i)))
        @pl.when(own)
        def _():
            pl.semaphore_wait(barrier, 33)

        @pl.when(jnp.logical_not(own))
        def _():
            pl.semaphore_wait(barrier, 35)

    @pl.when(jnp.logical_not(active))
    def _():
        pl.semaphore_wait(barrier, 19)

    def hop_a(m):
        copy(a_ref.at[m, head_row(x)], l1a.at[x, m], r_a1.at[x, m])

        def one(j):
            xx, to = along_x(j)
            send(a_ref.at[m, head_row(xx)], l1a.at[x, m], s_a1, r_a1.at[x, m], to)

        loop(1, 4, one)

    def hops_a():
        loop(0, 3, lambda j: hop_a((j + z_lo) % 3))

    hops_a()

    copy(g_ref, gn.at[x], r_gn)
    loop(1, 4, lambda j: send(g_ref, gn.at[x], s_gn, r_gn, along_x(j)[1]))
    def send_og(j):
        m = (j + z_lo) % 3
        send(og_ref.at[m, head_row(x)], og_s.at[z_lo], s_og, r_og, unit_device(m))

    loop(0, 3, send_og)
    gsum[...] = jnp.zeros_like(gsum)

    def forward_a(s):
        def one(j):
            m = (j + z_lo) % 3
            wait(l1a.at[s, m], r_a1.at[s, m])
            send(l1a.at[s, m], a_s.at[s, z_lo], s_a2.at[s], r_a2.at[s], unit_device(m))

        loop(0, 3, one)

    def hop_out(s, lo=0, hi=3):
        row = head_row(x)

        @pl.when(x == s)
        def _():
            def one(m):
                wait(l1o.at[s, m], r_o1.at[s, m])
                copy(l1o.at[s, m], out_ref.at[m, row], r_o2)

            loop(lo, hi, one)

        @pl.when(x != s)
        def _():
            def one(m):
                wait(l1o.at[s, m], r_o1.at[s, m])
                send(l1o.at[s, m], out_ref.at[m, row], s_o2.at[s], r_o2, dev(s, y, z_lo, z_hi, c))

            loop(lo, hi, one)

    def hop_gains(s):
        row = head_row(x)
        wait(gl1.at[s], r_p2.at[s])
        ghop[s] = jnp.sum(gl1[s], axis=1)

        @pl.when(x == s)
        def _():
            copy(ghop.at[s], gall.at[row], r_p3)

        @pl.when(x != s)
        def _():
            send(ghop.at[s], gall.at[row], s_p3.at[s], r_p3, dev(s, y, z_lo, z_hi, c))

    def share_gains(s):
        copy(gsum.at[s], gcol.at[s, d], r_p1.at[s])
        for _, to in peers():
            send(gsum.at[s], gcol.at[s, d], s_p1.at[s], r_p1.at[s], to)

    def unit_gains(s):
        wait(gcol.at[s], r_p1.at[s])
        gunit[s] = jnp.sum(gcol[s], axis=0)

        def one(i):
            at = gl1.at[s, u_m, z_hi * 2 + u_c]
            for to in sample_frames(i):
                @pl.when(is_me(to))
                def _():
                    copy(gunit.at[s], at, r_p2.at[s])

                @pl.when(jnp.logical_not(is_me(to)))
                def _():
                    send(gunit.at[s], at, s_p2.at[s], r_p2.at[s], to)

        loop(0, 4, one)

    def send_out(s, lo, hi):
        loop(lo, hi, lambda i: send(
            dxs.at[s, i], l1o.at[s, u_m], s_o1.at[s], r_o1.at[s, u_m],
            frame_device(i)))

    def to_tokens(src, dst, ssem, rsem, first=0, frames=4):
        fr = pl.ds(first, frames)

        def rows(p):
            return src.at[fr, pl.ds(pl.multiple_of(p * 32, 32), 32), :]

        copy(rows(d), dst.at[d, fr], rsem)

        for p, to in peers():
            send(rows(p), dst.at[d, fr], ssem, rsem, to)

    def to_frames(src, dst, ssem, rsem, first):
        mine = pl.ds(pl.multiple_of(d * 32 + first, 16), 16)
        part = pl.ds(first, 16)
        copy(src.at[d, :, part, :], dst.at[:, mine, :], rsem)

        for p, to in peers():
            send(src.at[p, :, part, :], dst.at[:, mine, :], ssem, rsem, to)

    def gain_row(s, l, j):
        return gn[s, l, u_h, j:j + 1, :]

    def spatial_fwd(s):
        gq, gk = gain_row(s, 0, 0), gain_row(s, 0, 1)
        b = s % 2
        for i in range(4):
            ab = a_s[s, i]
            u = ab.astype(F32)
            (r,), (n,), (q,), (k,), (p,) = attend_fwd([u], gq, gk, None)
            pb = p.astype(BF)
            sp[b, i] = p
            spb[b, i] = pb
            sq[b, i] = q
            sk[b, i] = k
            sn[b, i] = n
            sr[b, i] = jnp.broadcast_to(r, n.shape)
            ys[s, i] = (u + dot(pb, ab, 0, 0)).astype(BF)

    def add_gains(s, l, dgq, dgk):
        gsum[s, 2 * l:2 * l + 1, :] += dgq
        gsum[s, 2 * l + 1:2 * l + 2, :] += dgk

    def spatial_bwd(s, first):
        gq, gk = gain_row(s, 0, 0), gain_row(s, 0, 1)
        b = s % 2
        two = (first, first + 1)
        dx, dgq, dgk = attend_bwd(
            [(dys[s, i], a_s[s, i], sp[b, i], spb[b, i], sq[b, i], sk[b, i], sn[b, i], sr[b, i])
             for i in two], gq, gk)
        for i, block in zip(two, dx):
            dxs[s, i] = block.astype(BF)
        add_gains(s, 0, dgq, dgk)

    ri = lax.broadcasted_iota(jnp.int32, (128, 128), 0)
    ci = lax.broadcasted_iota(jnp.int32, (128, 128), 1)
    same = (ri // 32) == (ci // 32)

    def by_token(src):
        xf[...] = src[...].reshape(FRAMES * 32, HD).astype(F32)

    def token_rows(b):
        return jnp.concatenate(
            [xf[pl.ds(b * 4 + t, FRAMES, stride=32), :] for t in range(4)], axis=0)

    def temporal_fwd(s):
        by_token(yt.at[s])
        gq, gk = gain_row(s, 1, 0), gain_row(s, 1, 1)
        for first in range(0, 8, 4):
            four = range(first, first + 4)
            us = [token_rows(b) for b in four]
            for b, u, r, n, q, k, p in zip(four, us, *attend_fwd(us, gq, gk, same)):
                tx[b] = u.astype(BF)
                tp[b] = p
                tpb[b] = p.astype(BF)
                tq[b] = q
                tk[b] = k
                tn[b] = n
                trr[b] = jnp.broadcast_to(r, n.shape)

    def temporal_bwd(s, first):
        gq, gk = gain_row(s, 1, 0), gain_row(s, 1, 1)
        four = range(first, first + 4)
        dx, dgq, dgk = attend_bwd(
            [(token_rows(b).astype(BF), tx[b], tp[b], tpb[b], tq[b], tk[b], tn[b], trr[b])
             for b in four], gq, gk)
        for b, block in zip(four, dx):
            for t in range(4):
                xo[pl.ds(b * 4 + t, FRAMES, stride=32), :] = block[t * 32:(t + 1) * 32]
        add_gains(s, 1, dgq, dgk)
        part = slice(4 * first, 4 * first + 16)
        dyt[s, :, :, part, :] = xo.reshape(8, 4, 32, HD)[:, :, part, :].astype(BF)

    forward_a(last)

    @pl.when(active)
    def _():
        wait(og_s, r_og)
        to_tokens(og_s, gt.at[last], s_g.at[last], r_g.at[last])
        wait(gn, r_gn)
        wait(a_s.at[last], r_a2.at[last])
        spatial_fwd(last)
        to_tokens(ys.at[last], yt.at[last], s_y.at[last], r_y.at[last])
        loop(0, 4, lambda i: pl.semaphore_signal(
            go, inc=1, device_id=frame_device(i), device_id_type=MESH))
        forward_a(last - 1)
        wait(yt.at[last], r_y.at[last])
        temporal_fwd(last)

        def section(step):
            s = last - step
            before = jnp.maximum(s - 1, 0)
            after = jnp.minimum(s + 1, last)
            wait(gt.at[s], r_g.at[s])
            by_token(gt.at[s])
            for part in range(2):
                temporal_bwd(s, 4 * part)
                to_frames(dyt.at[s], dys.at[s], s_dy.at[s], r_dy.at[s], 16 * part)

            @pl.when(s > 1)
            def _():
                forward_a(jnp.maximum(s - 2, 0))

            @pl.when(s > 0)
            def _():
                wait(a_s.at[before], r_a2.at[before])
                spatial_fwd(before)
                to_tokens(ys.at[before], yt.at[before], s_y.at[before], r_y.at[before])

            @pl.when(s < last)
            def _():
                unit_gains(after)

            wait(dys.at[s], r_dy.at[s])

            @pl.when(s == 0)
            def _():
                hop_gains(3)
                hop_gains(2)

            spatial_bwd(s, 0)

            @pl.when(s > 0)
            def _():
                to_tokens(dxs.at[s], gt.at[before], s_g.at[before], r_g.at[before], 0, 2)

            @pl.when(s == 0)
            def _():
                send_out(s, 0, 2)

            spatial_bwd(s, 2)

            @pl.when(s > 0)
            def _():
                to_tokens(dxs.at[s], gt.at[before], s_g.at[before], r_g.at[before], 2, 2)
                wait(yt.at[before], r_y.at[before])
                temporal_fwd(before)

            share_gains(s)

            @pl.when(s > 0)
            def _():
                send_out(s, 0, 4)

            @pl.when(s == 0)
            def _():
                send_out(s, 2, 4)

        loop(0, SECTIONS, section)
        pl.semaphore_wait(go, 3)
        unit_gains(0)
        hop_gains(1)
        hop_out(3)
        hop_out(2)
        hop_out(1)

    @pl.when(jnp.logical_not(active))
    def _():
        wait(gn, r_gn)
        pl.semaphore_wait(go, 3)
        loop(1, SECTIONS, lambda j: forward_a(last - j))

        def relay(j):
            hop_out(last - j)
            hop_gains(last - j)

        loop(0, SECTIONS - 1, relay)

    hop_out(0)
    hop_gains(0)

    wait(gall, r_p3)
    for row in range(4):
        for m in range(3):
            for l in range(2):
                gout_ref[l, row + 4 * m] = gall[row, m, 2 * l:2 * l + 2]

    wait(out_ref, r_o2)

    wait(l1a.at[pl.ds(0, 3)], s_a1)
    wait(og_s.at[pl.ds(0, 3)], s_og)
    wait(gn.at[pl.ds(0, 3)], s_gn)

    def drain(s):
        wait(l1a.at[s], s_a2.at[s])

        @pl.when(x != s)
        def _():
            wait(l1o.at[s], s_o2.at[s])
            wait(ghop.at[s], s_p3.at[s])

    loop(0, SECTIONS, drain)

    @pl.when(active)
    def _():
        slots = gcol.reshape(32, 4, HD)

        def drain(s):
            wait(dyt.at[s, pl.ds(0, 7)], s_y.at[s])
            wait(dyt.at[s, pl.ds(0, 7)], s_g.at[s])
            wait(dyt.at[s, pl.ds(0, 7)], s_dy.at[s])
            wait(dxs.at[s], s_o1.at[s])
            wait(gcol.at[s, pl.ds(0, 7)], s_p1.at[s])

            @pl.when(own)
            def _():
                wait(slots.at[pl.ds(0, 15)], s_p2.at[s])

            @pl.when(jnp.logical_not(own))
            def _():
                wait(slots.at[pl.ds(0, 16)], s_p2.at[s])

        loop(0, SECTIONS, drain)


def hand_over(grads, gains, grads_out, gains_out, buf, gbuf, s_in, s_out):
    parts = [(grads.at[m], buf.at[m], grads_out.at[m]) for m in range(3)]
    parts.append((gains, gbuf, gains_out))
    first = [pltpu.make_async_copy(a, b, s_in.at[i]) for i, (a, b, _) in enumerate(parts)]
    second = [pltpu.make_async_copy(b, c, s_out.at[i]) for i, (_, b, c) in enumerate(parts)]
    for one in first:
        one.start()
    for one, other in zip(first, second):
        one.wait()
        other.start()
    for one in second:
        one.wait()


def per_device(section_inputs, out_grad, gains):
    def by_head(block):
        return block.reshape(TOKENS, HEADS, HD).transpose(1, 0, 2).reshape(3, 4, TOKENS, HD)

    a, og = by_head(section_inputs), by_head(out_grad)
    g = gains.reshape(2, 2, HEADS, HD).transpose(0, 2, 1, 3)
    V, D = pltpu.VMEM, pltpu.SemaphoreType.DMA
    s4, s43 = (SECTIONS,), (SECTIONS, 3)
    scratch = [
        V((4, 3, TOKENS, HD), BF),
        V((4, 4, TOKENS, HD), BF),
        V((4, TOKENS, HD), BF),
        V((4, 2, HEADS, 2, HD), F32),
        V((4, 4, TOKENS, HD), BF),
        V((4, 8, 4, 32, HD), BF),
        V((4, 8, 4, 32, HD), BF),
        V((4, 8, 4, 32, HD), BF),
        V((4, 4, TOKENS, HD), BF),
        V((4, 4, TOKENS, HD), BF),
        V((4, 3, TOKENS, HD), BF),
        V((FRAMES * 32, HD), F32),
        V((FRAMES * 32, HD), F32),
        V((2, 4, TOKENS, TOKENS), F32),
        V((2, 4, TOKENS, TOKENS), BF),
        V((2, 4, TOKENS, HD), BF),
        V((2, 4, TOKENS, HD), BF),
        V((2, 4, TOKENS, HD), F32),
        V((2, 4, TOKENS, HD), F32),
        V((8, 128, HD), BF),
        V((8, 128, 128), F32),
        V((8, 128, 128), BF),
        V((8, 128, HD), BF),
        V((8, 128, HD), BF),
        V((8, 128, HD), F32),
        V((8, 128, HD), F32),
        V((4, 4, HD), F32),
        V((4, 8, 4, HD), F32),
        V((4, 4, HD), F32),
        V((4, 3, 4, 4, HD), F32),
        V((4, 3, 4, HD), F32),
        V((4, 3, 4, HD), F32),
        D, D(s43), D(s4), D(s4), D, D, D, D, D(s4), D(s4), D(s4), D(s4), D(s4), D(s4),
        D(s4), D(s43), D(s4), D, D(s4), D(s4), D(s4), D(s4), D(s4), D, pltpu.SemaphoreType.REGULAR,
    ]
    vm = pl.BlockSpec(memory_space=pltpu.VMEM)
    hbm = pl.BlockSpec(memory_space=pl.ANY)
    grads, gain_grads = pl.pallas_call(
        kernel,
        out_shape=(
            jax.ShapeDtypeStruct((3, 4, TOKENS, HD), BF),
            jax.ShapeDtypeStruct((2, HEADS, 2, HD), F32),
        ),
        in_specs=[hbm, hbm, hbm],
        out_specs=(hbm, vm),
        scratch_shapes=scratch,
        compiler_params=pltpu.CompilerParams(
            has_side_effects=True, collective_id=0, vmem_limit_bytes=60 * 1024 * 1024),
        name="sections_back",
    )(a, og, g)
    grads, gain_grads = pl.pallas_call(
        hand_over,
        out_shape=(
            jax.ShapeDtypeStruct(grads.shape, BF),
            jax.ShapeDtypeStruct(gain_grads.shape, F32),
        ),
        in_specs=[hbm, hbm],
        out_specs=(hbm, hbm),
        scratch_shapes=[V(grads.shape, BF), V(gain_grads.shape, F32), D(s4), D(s4)],
        compiler_params=pltpu.CompilerParams(vmem_limit_bytes=60 * 1024 * 1024),
        name="hand_over",
    )(grads, gain_grads)
    grads = grads.reshape(HEADS, TOKENS, HD).transpose(1, 0, 2).reshape(section_inputs.shape)
    return grads, gain_grads.transpose(0, 2, 1, 3)[None]


def solution(mesh):
    return jax.shard_map(
        per_device,
        mesh=mesh,
        in_specs=(
            P("pipe", "dp", "seq", None, None, None),
            P("dp", "seq", None, None, None),
            P("pipe", None, None, None, None),
        ),
        out_specs=(P("pipe", "dp", "seq", None, None, None), P("pipe", None, None, None, None)),
        check_vma=False,
    )
```

```python
import jax
import jax.numpy as jnp
from jax import lax
from jax.experimental import pallas as pl
from jax.experimental.pallas import tpu as pltpu
from jax.sharding import PartitionSpec as P

MESH = pl.DeviceIdType.MESH
BF = jnp.bfloat16
F32 = jnp.float32
HEADS, HD, TOKENS, FRAMES, SECTIONS = 12, 128, 256, 32, 4
SCALE = HD ** -0.5
EXP2 = SCALE * 1.4426950408889634


def dot(a, b, ca, cb):
    return lax.dot_general(a, b, (((ca,), (cb,)), ((), ())), preferred_element_type=F32)


def attend_fwd(us, gain_q, gain_k, mask):
    rs = [lax.rsqrt(jnp.mean(u * u, axis=-1, keepdims=True) + 1e-06) for u in us]
    ns = [u * r for u, r in zip(us, rs)]
    qs = [(n * gain_q).astype(BF) for n in ns]
    ks = [(n * gain_k).astype(BF) for n in ns]
    ps = []
    for st in [dot(k, q, 1, 1) for k, q in zip(ks, qs)]:
        if mask is not None:
            st = jnp.where(mask, st, -1e30)
        top = jnp.max(st, axis=0, keepdims=True)
        e = jnp.exp2((st - top) * EXP2)
        ps.append(e * (1.0 / jnp.sum(e, axis=0, keepdims=True)))
    return rs, ns, qs, ks, ps


def attend_bwd(blocks, gain_q, gain_k):
    dps = [dot(u, do, 1, 1) for do, u, p, pb, q, k, n, r in blocks]
    dus = [dot(pb, do, 1, 0) for do, u, p, pb, q, k, n, r in blocks]
    dss = []
    for dp, (do, u, p, pb, q, k, n, r) in zip(dps, blocks):
        row = jnp.sum(p * dp, axis=0, keepdims=True)
        dss.append((p * (dp - row)).astype(BF))
    dks = [dot(ds, b[4], 1, 0) for ds, b in zip(dss, blocks)]
    dqs = [dot(ds, b[5], 0, 0) for ds, b in zip(dss, blocks)]
    dxs, gq, gk = [], 0.0, 0.0
    for dk, dq, du, (do, u, p, pb, q, k, n, r) in zip(dks, dqs, dus, blocks):
        dn = dq * (gain_q * SCALE) + dk * (gain_k * SCALE)
        along = jnp.mean(dn * n, axis=-1, keepdims=True)
        dxs.append(do.astype(F32) + du + r * (dn - n * along))
        gq = gq + jnp.sum(dq * n, axis=0, keepdims=True)
        gk = gk + jnp.sum(dk * n, axis=0, keepdims=True)
    return dxs, gq * SCALE, gk * SCALE


def kernel(a_ref, og_ref, g_ref, out_ref, gains_ref,
           l1a, a_s, og_s, gn, ys, yt, gt, dyt, dys, dxs, l1o,
           xf, xo, sp, spb, sq, sk, sn, sr, tx, tp, tpb, tq, tk, tn, trr,
           gsum, gcol, gunit,
           s_a1, r_a1, s_a2, r_a2, s_og, r_og, s_gn, r_gn, s_y, r_y, s_g, r_g, s_dy, r_dy,
           s_o1, r_o1, s_o2, r_o2, s_p1, r_p1, s_p2, r_p2, go, go_first):
    seq = lax.axis_index("seq")
    x = lax.axis_index("pipe")
    dp_i = lax.axis_index("dp")
    z_lo, y = seq // 8, seq % 8
    z_hi, c = dp_i // 2, dp_i % 2
    half, yy = y // 4, y % 4
    rest = (yy + 3 - z_lo) % 4
    active = rest < 3
    u_c = half
    u_m = jnp.minimum(rest, 2)
    u_r = (z_lo + 4 - u_m) % 4
    u_h = u_r + 4 * u_m
    d = x * 2 + c
    last = SECTIONS - 1

    def dev(xx, y_, zl, zh, cc):
        return {"seq": zl * 8 + y_, "pipe": xx, "dp": zh * 2 + cc}

    def send(src, dst, ssem, rsem, to):
        pltpu.make_async_remote_copy(
            src_ref=src, dst_ref=dst, send_sem=ssem, recv_sem=rsem,
            device_id=to, device_id_type=MESH,
        ).start()

    def copy(src, dst, sem):
        pltpu.make_async_copy(src, dst, sem).start()

    def wait(ref, sem):
        pltpu.make_async_copy(ref, ref, sem).wait()

    def loop(lo, hi, body):
        def step(i, _):
            body(i)
            return 0

        lax.fori_loop(lo, hi, step, 0)

    def head_row(plane):
        return (plane + 4 - yy + z_lo) % 4

    def unit_device(m):
        zl = (head_row(x) + m) % 4
        return dev(x, 4 * c + (zl + 1 + m) % 4, zl, z_hi, (half + 1) % 2)

    def frame_device(i):
        return dev(x, (x + i + 4 - u_r) % 4 + 4 * ((c + 1) % 2), i, z_hi, u_c)

    def first_frame(i):
        return dev(0, (x + i + 4 - u_r) % 4 + 4 * ((c + 1) % 2), i, z_hi, u_c)

    def peers():
        for dx in (2, 1, 3, 0):
            for cc in (c, 1 - c) if dx else (1 - c,):
                xx = (x + dx) % 4
                yield xx * 2 + cc, dev(xx, y, z_lo, z_hi, cc)

    def along_x(j):
        xx = (x + j) % 4
        return xx, dev(xx, y, z_lo, z_hi, c)

    def sample_frames(s, i):
        y_f = (x + i + 4 - u_r) % 4 + 4 * ((c + 1) % 2)
        for zh in range(2):
            for cc in range(2):
                yield dev(s, y_f, i, zh, cc)

    barrier = pltpu.get_barrier_semaphore()

    def greet(to):
        pl.semaphore_signal(barrier, inc=1, device_id=to, device_id_type=MESH)

    for _, to in peers():
        greet(to)

    loop(0, 3, lambda m: greet(unit_device(m)))
    greet(dev(x, y, z_lo, 1 - z_hi, c))
    greet(dev(x, y, z_lo, 1 - z_hi, 1 - c))

    @pl.when(active)
    def _():
        loop(0, 4, lambda i: greet(frame_device(i)))

    pl.semaphore_wait(barrier, 12 + 4 * active.astype(jnp.int32))

    def is_me(to):
        return (to["seq"] == seq) & (to["pipe"] == x) & (to["dp"] == dp_i)

    own = (x + z_lo + 4 - u_r) % 4 + 4 * ((c + 1) % 2) == y

    def hop_a(m):
        copy(a_ref.at[m, head_row(x)], l1a.at[x, m], r_a1.at[x, m])

        def one(j):
            xx, to = along_x(j)
            send(a_ref.at[m, head_row(xx)], l1a.at[x, m], s_a1, r_a1.at[x, m], to)

        loop(1, 4, one)

    def hops_a():
        loop(0, 3, lambda j: hop_a((j + z_lo) % 3))

    @pl.when(jnp.logical_or(x == last, jnp.logical_not(active)))
    def _():
        hops_a()

    copy(g_ref, gn.at[x], r_gn)
    loop(1, 4, lambda j: send(g_ref, gn.at[x], s_gn, r_gn, along_x(j)[1]))
    def send_og(j):
        m = (j + z_lo) % 3
        send(og_ref.at[m, head_row(x)], og_s.at[z_lo], s_og, r_og, unit_device(m))

    loop(0, 3, send_og)
    gsum[...] = jnp.zeros_like(gsum)

    def forward_a(s, then=None):
        def one(j):
            m = (j + z_lo) % 3
            wait(l1a.at[s, m], r_a1.at[s, m])
            send(l1a.at[s, m], a_s.at[s, z_lo], s_a2.at[s], r_a2.at[s], unit_device(m))

        if then is None:
            loop(0, 3, one)
        else:
            one(0)
            then()
            loop(1, 3, one)

    def hop_out(s, lo=0, hi=3):
        row = head_row(x)

        @pl.when(x == s)
        def _():
            def one(m):
                wait(l1o.at[s, m], r_o1.at[s, m])
                copy(l1o.at[s, m], out_ref.at[m, row], r_o2)

            loop(lo, hi, one)

        @pl.when(x != s)
        def _():
            def one(m):
                wait(l1o.at[s, m], r_o1.at[s, m])
                send(l1o.at[s, m], out_ref.at[m, row], s_o2.at[s], r_o2, dev(s, y, z_lo, z_hi, c))

            loop(lo, hi, one)

    def share_gains(s):
        copy(gsum.at[s], gcol.at[s, d], r_p1.at[s])
        for _, to in peers():
            send(gsum.at[s], gcol.at[s, d], s_p1.at[s], r_p1.at[s], to)

    def unit_gains(s):
        wait(gcol.at[s], r_p1.at[s])
        gunit[s] = jnp.sum(gcol[s], axis=0)

        def one(i):
            at = gains_ref.at[u_r, u_m, z_hi * 2 + u_c]
            for to in sample_frames(s, i):
                @pl.when(is_me(to))
                def _():
                    copy(gunit.at[s], at, r_p2)

                @pl.when(jnp.logical_not(is_me(to)))
                def _():
                    send(gunit.at[s], at, s_p2.at[s], r_p2, to)

        loop(0, 4, one)

    def send_first(lo, hi):
        loop(lo, hi, lambda i: send(
            dxs.at[0, i], out_ref.at[u_m, u_r], s_o1.at[0], r_o2, first_frame(i)))

    def ready_for_first():
        loop(0, 3, lambda m: pl.semaphore_signal(
            go_first, inc=1, device_id=unit_device(m), device_id_type=MESH))

    def send_out(s, lo, hi):
        loop(lo, hi, lambda i: send(
            dxs.at[s, i], l1o.at[s, u_m], s_o1.at[s], r_o1.at[s, u_m],
            frame_device(i)))

    def to_tokens(src, dst, ssem, rsem, first=0, frames=4):
        fr = pl.ds(first, frames)

        def rows(p):
            return src.at[fr, pl.ds(pl.multiple_of(p * 32, 32), 32), :]

        copy(rows(d), dst.at[d, fr], rsem)

        for p, to in peers():
            send(rows(p), dst.at[d, fr], ssem, rsem, to)

    def to_frames(src, dst, ssem, rsem, first):
        mine = pl.ds(pl.multiple_of(d * 32 + first, 16), 16)
        part = pl.ds(first, 16)
        copy(src.at[d, :, part, :], dst.at[:, mine, :], rsem)

        for p, to in peers():
            send(src.at[p, :, part, :], dst.at[:, mine, :], ssem, rsem, to)

    def gain_row(s, l, j):
        return gn[s, l, u_h, j:j + 1, :]

    def spatial_fwd(s, frames=range(4)):
        gq, gk = gain_row(s, 0, 0), gain_row(s, 0, 1)
        b = s % 2
        for i in frames:
            ab = a_s[s, i]
            u = ab.astype(F32)
            (r,), (n,), (q,), (k,), (p,) = attend_fwd([u], gq, gk, None)
            pb = p.astype(BF)
            sp[b, i] = p
            spb[b, i] = pb
            sq[b, i] = q
            sk[b, i] = k
            sn[b, i] = n
            sr[b, i] = jnp.broadcast_to(r, n.shape)
            ys[s, i] = (u + dot(pb, ab, 0, 0)).astype(BF)

    def add_gains(s, l, dgq, dgk):
        gsum[s, 2 * l:2 * l + 1, :] += dgq
        gsum[s, 2 * l + 1:2 * l + 2, :] += dgk

    def spatial_bwd(s, first):
        gq, gk = gain_row(s, 0, 0), gain_row(s, 0, 1)
        b = s % 2
        two = (first, first + 1)
        dx, dgq, dgk = attend_bwd(
            [(dys[s, i], a_s[s, i], sp[b, i], spb[b, i], sq[b, i], sk[b, i], sn[b, i], sr[b, i])
             for i in two], gq, gk)
        for i, block in zip(two, dx):
            dxs[s, i] = block.astype(BF)
        add_gains(s, 0, dgq, dgk)

    ri = lax.broadcasted_iota(jnp.int32, (128, 128), 0)
    ci = lax.broadcasted_iota(jnp.int32, (128, 128), 1)
    same = (ri // 32) == (ci // 32)

    def by_token(src):
        xf[...] = src[...].reshape(FRAMES * 32, HD).astype(F32)

    def token_rows(b):
        return jnp.concatenate(
            [xf[pl.ds(b * 4 + t, FRAMES, stride=32), :] for t in range(4)], axis=0)

    def temporal_fwd(s):
        by_token(yt.at[s])
        gq, gk = gain_row(s, 1, 0), gain_row(s, 1, 1)
        for first in range(0, 8, 4):
            four = range(first, first + 4)
            us = [token_rows(b) for b in four]
            for b, u, r, n, q, k, p in zip(four, us, *attend_fwd(us, gq, gk, same)):
                tx[b] = u.astype(BF)
                tp[b] = p
                tpb[b] = p.astype(BF)
                tq[b] = q
                tk[b] = k
                tn[b] = n
                trr[b] = jnp.broadcast_to(r, n.shape)

    def temporal_bwd(s, first):
        gq, gk = gain_row(s, 1, 0), gain_row(s, 1, 1)
        four = range(first, first + 4)
        dx, dgq, dgk = attend_bwd(
            [(token_rows(b).astype(BF), tx[b], tp[b], tpb[b], tq[b], tk[b], tn[b], trr[b])
             for b in four], gq, gk)
        for b, block in zip(four, dx):
            for t in range(4):
                xo[pl.ds(b * 4 + t, FRAMES, stride=32), :] = block[t * 32:(t + 1) * 32]
        add_gains(s, 1, dgq, dgk)
        part = slice(4 * first, 4 * first + 16)
        dyt[s, :, :, part, :] = xo.reshape(8, 4, 32, HD)[:, :, part, :].astype(BF)

    def follow():
        @pl.when(jnp.logical_and(x != last, active))
        def _():
            hops_a()

    forward_a(last, follow)

    @pl.when(active)
    def _():
        wait(og_s, r_og)
        to_tokens(og_s, gt.at[last], s_g.at[last], r_g.at[last])
        wait(gn, r_gn)
        wait(a_s.at[last], r_a2.at[last])
        for part in range(2):
            spatial_fwd(last, range(2 * part, 2 * part + 2))
            to_tokens(ys.at[last], yt.at[last], s_y.at[last], r_y.at[last], 2 * part, 2)

        loop(0, 4, lambda i: pl.semaphore_signal(
            go, inc=1, device_id=frame_device(i), device_id_type=MESH))
        forward_a(last - 1)
        wait(yt.at[last], r_y.at[last])
        temporal_fwd(last)

        def section(step):
            s = last - step
            before = jnp.maximum(s - 1, 0)
            after = jnp.minimum(s + 1, last)
            wait(gt.at[s], r_g.at[s])
            by_token(gt.at[s])
            for part in range(2):
                temporal_bwd(s, 4 * part)
                to_frames(dyt.at[s], dys.at[s], s_dy.at[s], r_dy.at[s], 16 * part)

            @pl.when(s > 1)
            def _():
                forward_a(jnp.maximum(s - 2, 0))

            @pl.when(s > 0)
            def _():
                wait(a_s.at[before], r_a2.at[before])
                spatial_fwd(before)
                to_tokens(ys.at[before], yt.at[before], s_y.at[before], r_y.at[before])

            @pl.when(s < last)
            def _():
                unit_gains(after)

            wait(dys.at[s], r_dy.at[s])

            @pl.when(s == 0)
            def _():
                ready_for_first()

            spatial_bwd(s, 0)

            @pl.when(s > 0)
            def _():
                to_tokens(dxs.at[s], gt.at[before], s_g.at[before], r_g.at[before], 0, 2)

            spatial_bwd(s, 2)

            @pl.when(s > 0)
            def _():
                to_tokens(dxs.at[s], gt.at[before], s_g.at[before], r_g.at[before], 2, 2)
                wait(yt.at[before], r_y.at[before])
                temporal_fwd(before)

            share_gains(s)

            @pl.when(s > 0)
            def _():
                send_out(s, 0, 4)

        loop(0, SECTIONS, section)
        pl.semaphore_wait(go, 3)
        hop_out(3)
        pl.semaphore_wait(go_first, 4)
        send_first(0, 4)
        unit_gains(0)
        hop_out(2)
        hop_out(1)

    @pl.when(jnp.logical_not(active))
    def _():
        ready_for_first()
        wait(gn, r_gn)
        pl.semaphore_wait(go, 3)
        loop(1, SECTIONS, lambda j: forward_a(last - j))

        loop(0, SECTIONS - 1, lambda j: hop_out(last - j))

    wait(l1a.at[pl.ds(0, 3)], s_a1)
    wait(og_s.at[pl.ds(0, 3)], s_og)
    wait(gn.at[pl.ds(0, 3)], s_gn)

    loop(0, SECTIONS, lambda s: wait(l1a.at[s], s_a2.at[s]))

    @pl.when(active)
    def _():
        slots = gcol.reshape(32, 4, HD)

        def drain(s):
            wait(dyt.at[s, pl.ds(0, 7)], s_y.at[s])
            wait(dyt.at[s, pl.ds(0, 7)], s_g.at[s])
            wait(dyt.at[s, pl.ds(0, 7)], s_dy.at[s])

            @pl.when(s > 0)
            def _():
                wait(dxs.at[s], s_o1.at[s])

            wait(gcol.at[s, pl.ds(0, 7)], s_p1.at[s])

            @pl.when(own & (s == x))
            def _():
                wait(slots.at[pl.ds(0, 15)], s_p2.at[s])

            @pl.when(jnp.logical_not(own & (s == x)))
            def _():
                wait(slots.at[pl.ds(0, 16)], s_p2.at[s])

        loop(0, SECTIONS, drain)

    wait(gains_ref, r_p2)
    wait(out_ref, r_o2)

    def drain(s):
        @pl.when(x != s)
        def _():
            wait(l1o.at[s], s_o2.at[s])

    loop(1, SECTIONS, drain)

    @pl.when(active)
    def _():
        wait(dxs.at[0], s_o1.at[0])


def hand_over(grads, gains, grads_out, gains_out, buf, gin, gbuf, s_in, s_out, s_g):
    parts = [(m, row) for m in range(3) for row in range(4)]
    first = [pltpu.make_async_copy(grads.at[p], buf.at[p], s_in.at[p]) for p in parts]
    second = [pltpu.make_async_copy(buf.at[p], grads_out.at[p], s_out.at[p]) for p in parts]
    arrive = pltpu.make_async_copy(gains, gin, s_g.at[0])
    leave = pltpu.make_async_copy(gbuf, gains_out, s_g.at[1])
    arrive.start()
    for one in first:
        one.start()
    arrive.wait()
    for m, row in parts:
        total = jnp.sum(gin[row, m], axis=0)
        for l in range(2):
            gbuf[l, row + 4 * m] = total[2 * l:2 * l + 2]
    leave.start()
    for one, other in zip(first, second):
        one.wait()
        other.start()
    leave.wait()
    for one in second:
        one.wait()


def per_device(section_inputs, out_grad, gains):
    def by_head(block):
        return block.reshape(TOKENS, HEADS, HD).transpose(1, 0, 2).reshape(3, 4, TOKENS, HD)

    a, og = by_head(section_inputs), by_head(out_grad)
    g = gains.reshape(2, 2, HEADS, HD).transpose(0, 2, 1, 3)
    V, D = pltpu.VMEM, pltpu.SemaphoreType.DMA
    s4, s43 = (SECTIONS,), (SECTIONS, 3)
    scratch = [
        V((4, 3, TOKENS, HD), BF),
        V((4, 4, TOKENS, HD), BF),
        V((4, TOKENS, HD), BF),
        V((4, 2, HEADS, 2, HD), F32),
        V((4, 4, TOKENS, HD), BF),
        V((4, 8, 4, 32, HD), BF),
        V((4, 8, 4, 32, HD), BF),
        V((4, 8, 4, 32, HD), BF),
        V((4, 4, TOKENS, HD), BF),
        V((4, 4, TOKENS, HD), BF),
        V((4, 3, TOKENS, HD), BF),
        V((FRAMES * 32, HD), F32),
        V((FRAMES * 32, HD), F32),
        V((2, 4, TOKENS, TOKENS), F32),
        V((2, 4, TOKENS, TOKENS), BF),
        V((2, 4, TOKENS, HD), BF),
        V((2, 4, TOKENS, HD), BF),
        V((2, 4, TOKENS, HD), F32),
        V((2, 4, TOKENS, HD), F32),
        V((8, 128, HD), BF),
        V((8, 128, 128), F32),
        V((8, 128, 128), BF),
        V((8, 128, HD), BF),
        V((8, 128, HD), BF),
        V((8, 128, HD), F32),
        V((8, 128, HD), F32),
        V((4, 4, HD), F32),
        V((4, 8, 4, HD), F32),
        V((4, 4, HD), F32),
        D, D(s43), D(s4), D(s4), D, D, D, D, D(s4), D(s4), D(s4), D(s4), D(s4), D(s4),
        D(s4), D(s43), D(s4), D, D(s4), D(s4), D(s4), D, pltpu.SemaphoreType.REGULAR, pltpu.SemaphoreType.REGULAR,
    ]
    hbm = pl.BlockSpec(memory_space=pl.ANY)
    grads, gain_grads = pl.pallas_call(
        kernel,
        out_shape=(
            jax.ShapeDtypeStruct((3, 4, TOKENS, HD), BF),
            jax.ShapeDtypeStruct((4, 3, 4, 4, HD), F32),
        ),
        in_specs=[hbm, hbm, hbm],
        out_specs=(hbm, hbm),
        scratch_shapes=scratch,
        compiler_params=pltpu.CompilerParams(
            has_side_effects=True, collective_id=0, vmem_limit_bytes=60 * 1024 * 1024),
        name="sections_back",
    )(a, og, g)
    grads, gain_grads = pl.pallas_call(
        hand_over,
        out_shape=(
            jax.ShapeDtypeStruct(grads.shape, BF),
            jax.ShapeDtypeStruct((2, HEADS, 2, HD), F32),
        ),
        in_specs=[hbm, hbm],
        out_specs=(hbm, hbm),
        scratch_shapes=[V(grads.shape, BF), V(gain_grads.shape, F32),
                        V((2, HEADS, 2, HD), F32), D((3, 4)), D((3, 4)), D((2,))],
        compiler_params=pltpu.CompilerParams(vmem_limit_bytes=60 * 1024 * 1024),
        name="hand_over",
    )(grads, gain_grads)
    grads = grads.reshape(HEADS, TOKENS, HD).transpose(1, 0, 2).reshape(section_inputs.shape)
    return grads, gain_grads.transpose(0, 2, 1, 3)[None]


def solution(mesh):
    return jax.shard_map(
        per_device,
        mesh=mesh,
        in_specs=(
            P("pipe", "dp", "seq", None, None, None),
            P("dp", "seq", None, None, None),
            P("pipe", None, None, None, None),
        ),
        out_specs=(P("pipe", "dp", "seq", None, None, None), P("pipe", None, None, None, None)),
        check_vma=False,
    )
```

```python
import jax
import jax.numpy as jnp
from jax import lax
from jax.experimental import pallas as pl
from jax.experimental.pallas import tpu as pltpu
from jax.sharding import PartitionSpec as P

MESH = pl.DeviceIdType.MESH
BF = jnp.bfloat16
F32 = jnp.float32
HEADS, HD, TOKENS, FRAMES, SECTIONS = 12, 128, 256, 32, 4
SCALE = HD ** -0.5
EXP2 = SCALE * 1.4426950408889634


def dot(a, b, ca, cb):
    return lax.dot_general(a, b, (((ca,), (cb,)), ((), ())), preferred_element_type=F32)


def attend_fwd(us, gain_q, gain_k, mask):
    rs = [lax.rsqrt(jnp.mean(u * u, axis=-1, keepdims=True) + 1e-06) for u in us]
    ns = [u * r for u, r in zip(us, rs)]
    qs = [(n * gain_q).astype(BF) for n in ns]
    ks = [(n * gain_k).astype(BF) for n in ns]
    ps = []
    for st in [dot(k, q, 1, 1) for k, q in zip(ks, qs)]:
        if mask is not None:
            st = jnp.where(mask, st, -1e30)
        top = jnp.max(st, axis=0, keepdims=True)
        e = jnp.exp2((st - top) * EXP2)
        ps.append(e * (1.0 / jnp.sum(e, axis=0, keepdims=True)))
    return rs, ns, qs, ks, ps


def attend_bwd(blocks, gain_q, gain_k):
    dps = [dot(u, do, 1, 1) for do, u, p, pb, q, k, n, r in blocks]
    dus = [dot(pb, do, 1, 0) for do, u, p, pb, q, k, n, r in blocks]
    dss = []
    for dp, (do, u, p, pb, q, k, n, r) in zip(dps, blocks):
        row = jnp.sum(p * dp, axis=0, keepdims=True)
        dss.append((p * (dp - row)).astype(BF))
    dks = [dot(ds, b[4], 1, 0) for ds, b in zip(dss, blocks)]
    dqs = [dot(ds, b[5], 0, 0) for ds, b in zip(dss, blocks)]
    dxs, gq, gk = [], 0.0, 0.0
    for dk, dq, du, (do, u, p, pb, q, k, n, r) in zip(dks, dqs, dus, blocks):
        dn = dq * (gain_q * SCALE) + dk * (gain_k * SCALE)
        along = jnp.mean(dn * n, axis=-1, keepdims=True)
        dxs.append(do.astype(F32) + du + r * (dn - n * along))
        gq = gq + jnp.sum(dq * n, axis=0, keepdims=True)
        gk = gk + jnp.sum(dk * n, axis=0, keepdims=True)
    return dxs, gq * SCALE, gk * SCALE


def kernel(a_ref, og_ref, g_ref, out_ref, gains_ref,
           l1a, a_s, og_s, gn, ys, yt, gt, dyt, dys, dxs, l1o,
           xf, xo, sp, spb, sq, sk, sn, sr, tx, tp, tpb, tq, tk, tn, trr,
           gsum, gcol, gunit,
           s_a1, r_a1, s_a2, r_a2, s_og, r_og, s_gn, r_gn, s_y, r_y, s_g, r_g, s_dy, r_dy,
           s_o1, r_o1, s_o2, r_o2, s_p1, r_p1, s_p2, r_p2, go, go_first):
    seq = lax.axis_index("seq")
    x = lax.axis_index("pipe")
    dp_i = lax.axis_index("dp")
    z_lo, y = seq // 8, seq % 8
    z_hi, c = dp_i // 2, dp_i % 2
    half, yy = y // 4, y % 4
    rest = (yy + 3 - z_lo) % 4
    active = rest < 3
    u_c = half
    u_m = jnp.minimum(rest, 2)
    u_r = (z_lo + 4 - u_m) % 4
    u_h = u_r + 4 * u_m
    d = x * 2 + c
    last = SECTIONS - 1

    def dev(xx, y_, zl, zh, cc):
        return {"seq": zl * 8 + y_, "pipe": xx, "dp": zh * 2 + cc}

    def send(src, dst, ssem, rsem, to):
        pltpu.make_async_remote_copy(
            src_ref=src, dst_ref=dst, send_sem=ssem, recv_sem=rsem,
            device_id=to, device_id_type=MESH,
        ).start()

    def copy(src, dst, sem):
        pltpu.make_async_copy(src, dst, sem).start()

    def wait(ref, sem):
        pltpu.make_async_copy(ref, ref, sem).wait()

    def loop(lo, hi, body):
        def step(i, _):
            body(i)
            return 0

        lax.fori_loop(lo, hi, step, 0)

    def head_row(plane):
        return (plane + 4 - yy + z_lo) % 4

    def unit_device(m):
        zl = (head_row(x) + m) % 4
        return dev(x, 4 * c + (zl + 1 + m) % 4, zl, z_hi, (half + 1) % 2)

    def frame_device(i):
        return dev(x, (x + i + 4 - u_r) % 4 + 4 * ((c + 1) % 2), i, z_hi, u_c)

    def first_frame(i):
        return dev(0, (x + i + 4 - u_r) % 4 + 4 * ((c + 1) % 2), i, z_hi, u_c)

    def peers():
        for dx in (2, 1, 3, 0):
            for cc in (c, 1 - c) if dx else (1 - c,):
                xx = (x + dx) % 4
                yield xx * 2 + cc, dev(xx, y, z_lo, z_hi, cc)

    def along_x(j):
        xx = (x + j) % 4
        return xx, dev(xx, y, z_lo, z_hi, c)

    def sample_frames(s, i):
        y_f = (x + i + 4 - u_r) % 4 + 4 * ((c + 1) % 2)
        for zh in range(2):
            for cc in range(2):
                yield dev(s, y_f, i, zh, cc)

    barrier = pltpu.get_barrier_semaphore()

    def greet(to):
        pl.semaphore_signal(barrier, inc=1, device_id=to, device_id_type=MESH)

    for _, to in peers():
        greet(to)

    loop(0, 3, lambda m: greet(unit_device(m)))
    greet(dev(x, y, z_lo, 1 - z_hi, c))
    greet(dev(x, y, z_lo, 1 - z_hi, 1 - c))

    @pl.when(active)
    def _():
        loop(0, 4, lambda i: greet(frame_device(i)))

    pl.semaphore_wait(barrier, 12 + 4 * active.astype(jnp.int32))

    def is_me(to):
        return (to["seq"] == seq) & (to["pipe"] == x) & (to["dp"] == dp_i)

    own = (x + z_lo + 4 - u_r) % 4 + 4 * ((c + 1) % 2) == y

    def piece(q):
        m = (q // 2 + z_lo) % 3
        return m, pl.ds(pl.multiple_of(q % 2 * 128, 128), 128), 2 * m + q % 2

    def hops_a():
        def one(q):
            m, rows, k = piece(q)
            copy(a_ref.at[m, head_row(x), rows], l1a.at[x, m, rows], r_a1.at[x, k])

            def to_plane(j):
                xx, to = along_x(j)
                send(a_ref.at[m, head_row(xx), rows], l1a.at[x, m, rows], s_a1, r_a1.at[x, k], to)

            loop(1, 4, to_plane)

        loop(0, 6, one)

    @pl.when(jnp.logical_or(x == last, jnp.logical_not(active)))
    def _():
        hops_a()

    copy(g_ref, gn.at[x], r_gn)
    loop(1, 4, lambda j: send(g_ref, gn.at[x], s_gn, r_gn, along_x(j)[1]))
    def send_og(j):
        m = (j + z_lo) % 3
        send(og_ref.at[m, head_row(x)], og_s.at[z_lo], s_og, r_og, unit_device(m))

    loop(0, 3, send_og)
    gsum[...] = jnp.zeros_like(gsum)

    def forward_a(s, then=None):
        def one(q):
            m, rows, k = piece(q)
            wait(l1a.at[s, m, rows], r_a1.at[s, k])
            send(l1a.at[s, m, rows], a_s.at[s, z_lo, rows], s_a2.at[s], r_a2.at[s],
                 unit_device(m))

        if then is None:
            loop(0, 6, one)
        else:
            loop(0, 2, one)
            then()
            loop(2, 6, one)

    def hop_out(s, lo=0, hi=3):
        row = head_row(x)

        @pl.when(x == s)
        def _():
            def one(m):
                wait(l1o.at[s, m], r_o1.at[s, m])
                copy(l1o.at[s, m], out_ref.at[m, row], r_o2)

            loop(lo, hi, one)

        @pl.when(x != s)
        def _():
            def one(m):
                wait(l1o.at[s, m], r_o1.at[s, m])
                send(l1o.at[s, m], out_ref.at[m, row], s_o2.at[s], r_o2, dev(s, y, z_lo, z_hi, c))

            loop(lo, hi, one)

    def share_gains(s):
        copy(gsum.at[s], gcol.at[s, d], r_p1.at[s])
        for _, to in peers():
            send(gsum.at[s], gcol.at[s, d], s_p1.at[s], r_p1.at[s], to)

    def unit_gains(s):
        wait(gcol.at[s], r_p1.at[s])
        gunit[s] = jnp.sum(gcol[s], axis=0)

        def one(i):
            at = gains_ref.at[u_r, u_m, z_hi * 2 + u_c]
            for to in sample_frames(s, i):
                @pl.when(is_me(to))
                def _():
                    copy(gunit.at[s], at, r_p2)

                @pl.when(jnp.logical_not(is_me(to)))
                def _():
                    send(gunit.at[s], at, s_p2.at[s], r_p2, to)

        loop(0, 4, one)

    def send_first(lo, hi):
        loop(lo, hi, lambda i: send(
            dxs.at[0, i], out_ref.at[u_m, u_r], s_o1.at[0], r_o2, first_frame(i)))

    def ready_for_first():
        loop(0, 3, lambda m: pl.semaphore_signal(
            go_first, inc=1, device_id=unit_device(m), device_id_type=MESH))

    def send_out(s, lo, hi):
        loop(lo, hi, lambda i: send(
            dxs.at[s, i], l1o.at[s, u_m], s_o1.at[s], r_o1.at[s, u_m],
            frame_device(i)))

    def to_tokens(src, dst, ssem, rsem, first=0, frames=4):
        fr = pl.ds(first, frames)

        def rows(p):
            return src.at[fr, pl.ds(pl.multiple_of(p * 32, 32), 32), :]

        copy(rows(d), dst.at[d, fr], rsem)

        for p, to in peers():
            send(rows(p), dst.at[d, fr], ssem, rsem, to)

    def to_frames(src, dst, ssem, rsem, first):
        mine = pl.ds(pl.multiple_of(d * 32 + first, 16), 16)
        copy(src.at[d], dst.at[:, mine, :], rsem)

        for p, to in peers():
            send(src.at[p], dst.at[:, mine, :], ssem, rsem, to)

    def gain_row(s, l, j):
        return gn[s, l, u_h, j:j + 1, :]

    def spatial_fwd(s, frames=range(4)):
        gq, gk = gain_row(s, 0, 0), gain_row(s, 0, 1)
        b = s % 2
        for i in frames:
            ab = a_s[s, i]
            u = ab.astype(F32)
            (r,), (n,), (q,), (k,), (p,) = attend_fwd([u], gq, gk, None)
            pb = p.astype(BF)
            sp[b, i] = p
            spb[b, i] = pb
            sq[b, i] = q
            sk[b, i] = k
            sn[b, i] = n
            sr[b, i] = jnp.broadcast_to(r, n.shape)
            ys[s, i] = (u + dot(pb, ab, 0, 0)).astype(BF)

    def add_gains(s, l, dgq, dgk):
        gsum[s, 2 * l:2 * l + 1, :] += dgq
        gsum[s, 2 * l + 1:2 * l + 2, :] += dgk

    def spatial_bwd(s, first):
        gq, gk = gain_row(s, 0, 0), gain_row(s, 0, 1)
        b = s % 2
        two = (first, first + 1)
        dx, dgq, dgk = attend_bwd(
            [(dys[s, i], a_s[s, i], sp[b, i], spb[b, i], sq[b, i], sk[b, i], sn[b, i], sr[b, i])
             for i in two], gq, gk)
        for i, block in zip(two, dx):
            dxs[s, i] = block.astype(BF)
        add_gains(s, 0, dgq, dgk)

    ri = lax.broadcasted_iota(jnp.int32, (128, 128), 0)
    ci = lax.broadcasted_iota(jnp.int32, (128, 128), 1)
    same = (ri // 32) == (ci // 32)

    def by_token(src):
        xf[...] = src[...].reshape(FRAMES * 32, HD).astype(F32)

    def token_rows(b):
        return jnp.concatenate(
            [xf[pl.ds(b * 4 + t, FRAMES, stride=32), :] for t in range(4)], axis=0)

    def temporal_fwd(s):
        by_token(yt.at[s])
        gq, gk = gain_row(s, 1, 0), gain_row(s, 1, 1)
        for first in range(0, 8, 4):
            four = range(first, first + 4)
            us = [token_rows(b) for b in four]
            for b, u, r, n, q, k, p in zip(four, us, *attend_fwd(us, gq, gk, same)):
                tx[b] = u.astype(BF)
                tp[b] = p
                tpb[b] = p.astype(BF)
                tq[b] = q
                tk[b] = k
                tn[b] = n
                trr[b] = jnp.broadcast_to(r, n.shape)

    def temporal_bwd(s, first):
        gq, gk = gain_row(s, 1, 0), gain_row(s, 1, 1)
        four = range(first, first + 4)
        dx, dgq, dgk = attend_bwd(
            [(token_rows(b).astype(BF), tx[b], tp[b], tpb[b], tq[b], tk[b], tn[b], trr[b])
             for b in four], gq, gk)
        for b, block in zip(four, dx):
            for t in range(4):
                xo[pl.ds((b - first) * 4 + t, FRAMES, stride=16), :] = block[t * 32:(t + 1) * 32]
        add_gains(s, 1, dgq, dgk)
        dyt[s, first // 4] = xo[...].astype(BF).reshape(8, 4, 16, HD)

    def follow():
        @pl.when(jnp.logical_and(x != last, active))
        def _():
            hops_a()

    forward_a(last, follow)

    @pl.when(active)
    def _():
        wait(og_s, r_og)
        to_tokens(og_s, gt.at[last], s_g.at[last], r_g.at[last])
        wait(gn, r_gn)
        wait(a_s.at[last], r_a2.at[last])
        for part in range(2):
            spatial_fwd(last, range(2 * part, 2 * part + 2))
            to_tokens(ys.at[last], yt.at[last], s_y.at[last], r_y.at[last], 2 * part, 2)

        loop(0, 4, lambda i: pl.semaphore_signal(
            go, inc=1, device_id=frame_device(i), device_id_type=MESH))
        forward_a(last - 1)
        wait(yt.at[last], r_y.at[last])
        temporal_fwd(last)

        def section(step):
            s = last - step
            before = jnp.maximum(s - 1, 0)
            after = jnp.minimum(s + 1, last)
            wait(gt.at[s], r_g.at[s])
            by_token(gt.at[s])
            for part in range(2):
                temporal_bwd(s, 4 * part)
                to_frames(dyt.at[s, part], dys.at[s], s_dy.at[s], r_dy.at[s, part], 16 * part)

            @pl.when(s > 1)
            def _():
                forward_a(jnp.maximum(s - 2, 0))

            @pl.when(s > 0)
            def _():
                wait(a_s.at[before], r_a2.at[before])
                spatial_fwd(before)
                to_tokens(ys.at[before], yt.at[before], s_y.at[before], r_y.at[before])

            @pl.when(s < last)
            def _():
                unit_gains(after)

            wait(dys.at[s, pl.ds(0, 2)], r_dy.at[s, 0])

            @pl.when(s == 0)
            def _():
                ready_for_first()

            wait(dys.at[s, pl.ds(2, 2)], r_dy.at[s, 1])
            spatial_bwd(s, 0)

            @pl.when(s > 0)
            def _():
                to_tokens(dxs.at[s], gt.at[before], s_g.at[before], r_g.at[before], 0, 2)

            spatial_bwd(s, 2)

            @pl.when(s > 0)
            def _():
                to_tokens(dxs.at[s], gt.at[before], s_g.at[before], r_g.at[before], 2, 2)
                wait(yt.at[before], r_y.at[before])
                temporal_fwd(before)

            share_gains(s)

            @pl.when(s > 0)
            def _():
                send_out(s, 0, 4)

        loop(0, SECTIONS, section)
        pl.semaphore_wait(go, 3)
        hop_out(3)
        hop_out(1)
        unit_gains(0)
        pl.semaphore_wait(go_first, 4)
        send_first(0, 4)
        hop_out(2)

    @pl.when(jnp.logical_not(active))
    def _():
        ready_for_first()
        wait(gn, r_gn)
        pl.semaphore_wait(go, 3)
        loop(1, SECTIONS, lambda j: forward_a(last - j))

        loop(0, SECTIONS - 1, lambda j: hop_out(last - j))

    wait(l1a.at[pl.ds(0, 3)], s_a1)
    wait(og_s.at[pl.ds(0, 3)], s_og)
    wait(gn.at[pl.ds(0, 3)], s_gn)

    loop(0, SECTIONS, lambda s: wait(l1a.at[s], s_a2.at[s]))

    @pl.when(active)
    def _():
        slots = gcol.reshape(32, 4, HD)

        def drain(s):
            wait(yt.at[s, pl.ds(0, 7)], s_y.at[s])
            wait(yt.at[s, pl.ds(0, 7)], s_g.at[s])
            wait(yt.at[s, pl.ds(0, 7)], s_dy.at[s])

            @pl.when(s > 0)
            def _():
                wait(dxs.at[s], s_o1.at[s])

            wait(gcol.at[s, pl.ds(0, 7)], s_p1.at[s])

            @pl.when(own & (s == x))
            def _():
                wait(slots.at[pl.ds(0, 15)], s_p2.at[s])

            @pl.when(jnp.logical_not(own & (s == x)))
            def _():
                wait(slots.at[pl.ds(0, 16)], s_p2.at[s])

        loop(0, SECTIONS, drain)

    wait(gains_ref, r_p2)
    wait(out_ref, r_o2)

    def drain(s):
        @pl.when(x != s)
        def _():
            wait(l1o.at[s], s_o2.at[s])

    loop(1, SECTIONS, drain)

    @pl.when(active)
    def _():
        wait(dxs.at[0], s_o1.at[0])


def hand_over(grads, gains, grads_out, gains_out, buf, gin, gbuf, s_in, s_out, s_g):
    first = [pltpu.make_async_copy(grads.at[m], buf.at[m], s_in.at[m]) for m in range(3)]
    second = [pltpu.make_async_copy(buf.at[m], grads_out.at[m], s_out.at[m]) for m in range(3)]
    arrive = pltpu.make_async_copy(gains, gin, s_g.at[0])
    leave = pltpu.make_async_copy(gbuf, gains_out, s_g.at[1])
    arrive.start()
    for one in first:
        one.start()
    arrive.wait()
    for row in range(4):
        for m in range(3):
            total = jnp.sum(gin[row, m], axis=0)
            for l in range(2):
                gbuf[l, row + 4 * m] = total[2 * l:2 * l + 2]
    leave.start()
    for one, other in zip(first, second):
        one.wait()
        other.start()
    leave.wait()
    for one in second:
        one.wait()


def per_device(section_inputs, out_grad, gains):
    def by_head(block):
        return block.reshape(TOKENS, HEADS, HD).transpose(1, 0, 2).reshape(3, 4, TOKENS, HD)

    a, og = by_head(section_inputs), by_head(out_grad)
    g = gains.reshape(2, 2, HEADS, HD).transpose(0, 2, 1, 3)
    V, D = pltpu.VMEM, pltpu.SemaphoreType.DMA
    s4, s43 = (SECTIONS,), (SECTIONS, 3)
    scratch = [
        V((4, 3, TOKENS, HD), BF),
        V((4, 4, TOKENS, HD), BF),
        V((4, TOKENS, HD), BF),
        V((4, 2, HEADS, 2, HD), F32),
        V((4, 4, TOKENS, HD), BF),
        V((4, 8, 4, 32, HD), BF),
        V((4, 8, 4, 32, HD), BF),
        V((4, 2, 8, 4, 16, HD), BF),
        V((4, 4, TOKENS, HD), BF),
        V((4, 4, TOKENS, HD), BF),
        V((4, 3, TOKENS, HD), BF),
        V((FRAMES * 32, HD), F32),
        V((FRAMES * 16, HD), F32),
        V((2, 4, TOKENS, TOKENS), F32),
        V((2, 4, TOKENS, TOKENS), BF),
        V((2, 4, TOKENS, HD), BF),
        V((2, 4, TOKENS, HD), BF),
        V((2, 4, TOKENS, HD), F32),
        V((2, 4, TOKENS, HD), F32),
        V((8, 128, HD), BF),
        V((8, 128, 128), F32),
        V((8, 128, 128), BF),
        V((8, 128, HD), BF),
        V((8, 128, HD), BF),
        V((8, 128, HD), F32),
        V((8, 128, HD), F32),
        V((4, 4, HD), F32),
        V((4, 8, 4, HD), F32),
        V((4, 4, HD), F32),
        D, D((SECTIONS, 6)), D(s4), D(s4), D, D, D, D, D(s4), D(s4), D(s4), D(s4), D(s4), D((SECTIONS, 2)),
        D(s4), D(s43), D(s4), D, D(s4), D(s4), D(s4), D, pltpu.SemaphoreType.REGULAR, pltpu.SemaphoreType.REGULAR,
    ]
    hbm = pl.BlockSpec(memory_space=pl.ANY)
    grads, gain_grads = pl.pallas_call(
        kernel,
        out_shape=(
            jax.ShapeDtypeStruct((3, 4, TOKENS, HD), BF),
            jax.ShapeDtypeStruct((4, 3, 4, 4, HD), F32),
        ),
        in_specs=[hbm, hbm, hbm],
        out_specs=(hbm, hbm),
        scratch_shapes=scratch,
        compiler_params=pltpu.CompilerParams(
            has_side_effects=True, collective_id=0, vmem_limit_bytes=60 * 1024 * 1024),
        name="sections_back",
    )(a, og, g)
    grads, gain_grads = pl.pallas_call(
        hand_over,
        out_shape=(
            jax.ShapeDtypeStruct(grads.shape, BF),
            jax.ShapeDtypeStruct((2, HEADS, 2, HD), F32),
        ),
        in_specs=[hbm, hbm],
        out_specs=(hbm, hbm),
        scratch_shapes=[V(grads.shape, BF), V(gain_grads.shape, F32),
                        V((2, HEADS, 2, HD), F32), D((3,)), D((3,)), D((2,))],
        compiler_params=pltpu.CompilerParams(vmem_limit_bytes=60 * 1024 * 1024),
        name="hand_over",
    )(grads, gain_grads)
    grads = grads.reshape(HEADS, TOKENS, HD).transpose(1, 0, 2).reshape(section_inputs.shape)
    return grads, gain_grads.transpose(0, 2, 1, 3)[None]


def solution(mesh):
    return jax.shard_map(
        per_device,
        mesh=mesh,
        in_specs=(
            P("pipe", "dp", "seq", None, None, None),
            P("dp", "seq", None, None, None),
            P("pipe", None, None, None, None),
        ),
        out_specs=(P("pipe", "dp", "seq", None, None, None), P("pipe", None, None, None, None)),
        check_vma=False,
    )
```

```python
import jax
import jax.numpy as jnp
from jax import lax
from jax.experimental import pallas as pl
from jax.experimental.pallas import tpu as pltpu
from jax.sharding import PartitionSpec as P

MESH = pl.DeviceIdType.MESH
BF = jnp.bfloat16
F32 = jnp.float32
HEADS, HD, TOKENS, FRAMES, SECTIONS = 12, 128, 256, 32, 4
SCALE = HD ** -0.5
EXP2 = SCALE * 1.4426950408889634


def dot(a, b, ca, cb):
    return lax.dot_general(a, b, (((ca,), (cb,)), ((), ())), preferred_element_type=F32)


def attend_fwd(us, gain_q, gain_k, mask):
    rs = [lax.rsqrt(jnp.mean(u * u, axis=-1, keepdims=True) + 1e-06) for u in us]
    ns = [u * r for u, r in zip(us, rs)]
    qs = [(n * gain_q).astype(BF) for n in ns]
    ks = [(n * gain_k).astype(BF) for n in ns]
    ps = []
    for st in [dot(k, q, 1, 1) for k, q in zip(ks, qs)]:
        if mask is not None:
            st = jnp.where(mask, st, -1e30)
        top = jnp.max(st, axis=0, keepdims=True)
        e = jnp.exp2((st - top) * EXP2)
        ps.append(e * (1.0 / jnp.sum(e, axis=0, keepdims=True)))
    return rs, ns, qs, ks, ps


def attend_bwd(blocks, gain_q, gain_k):
    dps = [dot(u, do, 1, 1) for do, u, p, pb, q, k, n, r in blocks]
    dus = [dot(pb, do, 1, 0) for do, u, p, pb, q, k, n, r in blocks]
    dss = []
    for dp, (do, u, p, pb, q, k, n, r) in zip(dps, blocks):
        row = jnp.sum(p * dp, axis=0, keepdims=True)
        dss.append((p * (dp - row)).astype(BF))
    dks = [dot(ds, b[4], 1, 0) for ds, b in zip(dss, blocks)]
    dqs = [dot(ds, b[5], 0, 0) for ds, b in zip(dss, blocks)]
    dxs, gq, gk = [], 0.0, 0.0
    for dk, dq, du, (do, u, p, pb, q, k, n, r) in zip(dks, dqs, dus, blocks):
        dn = dq * (gain_q * SCALE) + dk * (gain_k * SCALE)
        along = jnp.mean(dn * n, axis=-1, keepdims=True)
        dxs.append(do.astype(F32) + du + r * (dn - n * along))
        gq = gq + jnp.sum(dq * n, axis=0, keepdims=True)
        gk = gk + jnp.sum(dk * n, axis=0, keepdims=True)
    return dxs, gq * SCALE, gk * SCALE


def kernel(a_ref, og_ref, g_ref, out_ref, gains_ref,
           l1a, a_s, og_s, gn, ys, yt, gt, dyt, dys, dxs, l1o,
           xf, xo, sp, spb, sq, sk, sn, sr, tx, tp, tpb, tq, tk, tn, trr,
           gsum, gcol, gunit,
           s_a1, r_a1, s_a2, r_a2, s_og, r_og, s_gn, r_gn, s_y, r_y, s_g, r_g, s_dy, r_dy,
           s_o1, r_o1, s_o2, r_o2, s_p1, r_p1, s_p2, r_p2, go, go_first):
    seq = lax.axis_index("seq")
    x = lax.axis_index("pipe")
    dp_i = lax.axis_index("dp")
    z_lo, y = seq // 8, seq % 8
    z_hi, c = dp_i // 2, dp_i % 2
    half, yy = y // 4, y % 4
    rest = (yy + 3 - z_lo) % 4
    active = rest < 3
    u_c = half
    u_m = jnp.minimum(rest, 2)
    u_r = (z_lo + 4 - u_m) % 4
    u_h = u_r + 4 * u_m
    d = x * 2 + c
    last = SECTIONS - 1

    def dev(xx, y_, zl, zh, cc):
        return {"seq": zl * 8 + y_, "pipe": xx, "dp": zh * 2 + cc}

    def send(src, dst, ssem, rsem, to):
        pltpu.make_async_remote_copy(
            src_ref=src, dst_ref=dst, send_sem=ssem, recv_sem=rsem,
            device_id=to, device_id_type=MESH,
        ).start()

    def copy(src, dst, sem):
        pltpu.make_async_copy(src, dst, sem).start()

    def wait(ref, sem):
        pltpu.make_async_copy(ref, ref, sem).wait()

    def loop(lo, hi, body):
        def step(i, _):
            body(i)
            return 0

        lax.fori_loop(lo, hi, step, 0)

    def head_row(plane):
        return (plane + 4 - yy + z_lo) % 4

    def unit_device(m):
        zl = (head_row(x) + m) % 4
        return dev(x, 4 * c + (zl + 1 + m) % 4, zl, z_hi, (half + 1) % 2)

    def frame_device(i):
        return dev(x, (x + i + 4 - u_r) % 4 + 4 * ((c + 1) % 2), i, z_hi, u_c)

    def first_frame(i):
        return dev(0, (x + i + 4 - u_r) % 4 + 4 * ((c + 1) % 2), i, z_hi, u_c)

    def peers():
        for dx in (2, 1, 3, 0):
            for cc in (c, 1 - c) if dx else (1 - c,):
                xx = (x + dx) % 4
                yield xx * 2 + cc, dev(xx, y, z_lo, z_hi, cc)

    def along_x(j):
        xx = (x + j) % 4
        return xx, dev(xx, y, z_lo, z_hi, c)

    def sample_frames(s, i):
        y_f = (x + i + 4 - u_r) % 4 + 4 * ((c + 1) % 2)
        for zh in range(2):
            for cc in range(2):
                yield dev(s, y_f, i, zh, cc)

    barrier = pltpu.get_barrier_semaphore()

    def greet(to):
        pl.semaphore_signal(barrier, inc=1, device_id=to, device_id_type=MESH)

    for _, to in peers():
        greet(to)

    loop(0, 3, lambda m: greet(unit_device(m)))
    greet(dev(x, y, z_lo, 1 - z_hi, c))
    greet(dev(x, y, z_lo, 1 - z_hi, 1 - c))

    @pl.when(active)
    def _():
        loop(0, 4, lambda i: greet(frame_device(i)))

    pl.semaphore_wait(barrier, 12 + 4 * active.astype(jnp.int32))

    def is_me(to):
        return (to["seq"] == seq) & (to["pipe"] == x) & (to["dp"] == dp_i)

    own = (x + z_lo + 4 - u_r) % 4 + 4 * ((c + 1) % 2) == y

    def piece(q):
        m = (q // 2 + z_lo) % 3
        return m, pl.ds(pl.multiple_of(q % 2 * 128, 128), 128), 2 * m + q % 2

    def hops_a():
        def one(q):
            m, rows, k = piece(q)
            copy(a_ref.at[m, head_row(x), rows], l1a.at[x, m, rows], r_a1.at[x, k])

            def to_plane(j):
                xx, to = along_x(j)
                send(a_ref.at[m, head_row(xx), rows], l1a.at[x, m, rows], s_a1, r_a1.at[x, k], to)

            loop(1, 4, to_plane)

        loop(0, 6, one)

    @pl.when(jnp.logical_or(x == last, jnp.logical_not(active)))
    def _():
        hops_a()

    copy(g_ref, gn.at[x], r_gn)
    loop(1, 4, lambda j: send(g_ref, gn.at[x], s_gn, r_gn, along_x(j)[1]))
    def send_og(j):
        m = (j + z_lo) % 3
        send(og_ref.at[m, head_row(x)], og_s.at[z_lo], s_og, r_og, unit_device(m))

    loop(0, 3, send_og)
    gsum[...] = jnp.zeros_like(gsum)

    def forward_a(s, then=None):
        def one(q):
            m, rows, k = piece(q)
            wait(l1a.at[s, m, rows], r_a1.at[s, k])
            send(l1a.at[s, m, rows], a_s.at[s, z_lo, rows], s_a2.at[s], r_a2.at[s],
                 unit_device(m))

        if then is None:
            loop(0, 6, one)
        else:
            loop(0, 2, one)
            then()
            loop(2, 6, one)

    def hop_out(s, lo=0, hi=3):
        row = head_row(x)

        @pl.when(x == s)
        def _():
            def one(m):
                wait(l1o.at[s, m], r_o1.at[s, m])
                copy(l1o.at[s, m], out_ref.at[m, row], r_o2)

            loop(lo, hi, one)

        @pl.when(x != s)
        def _():
            def one(m):
                wait(l1o.at[s, m], r_o1.at[s, m])
                send(l1o.at[s, m], out_ref.at[m, row], s_o2.at[s], r_o2, dev(s, y, z_lo, z_hi, c))

            loop(lo, hi, one)

    def share_gains(s):
        copy(gsum.at[s], gcol.at[s, d], r_p1.at[s])
        for _, to in peers():
            send(gsum.at[s], gcol.at[s, d], s_p1.at[s], r_p1.at[s], to)

    def unit_gains(s):
        wait(gcol.at[s], r_p1.at[s])
        gunit[s] = jnp.sum(gcol[s], axis=0)

        def one(i):
            at = gains_ref.at[u_r, u_m, z_hi * 2 + u_c]
            for to in sample_frames(s, i):
                @pl.when(is_me(to))
                def _():
                    copy(gunit.at[s], at, r_p2)

                @pl.when(jnp.logical_not(is_me(to)))
                def _():
                    send(gunit.at[s], at, s_p2.at[s], r_p2, to)

        loop(0, 4, one)

    def send_first(lo, hi):
        loop(lo, hi, lambda i: send(
            dxs.at[0, i], out_ref.at[u_m, u_r], s_o1.at[0], r_o2, first_frame(i)))

    def next_frames(s):
        loop(0, 4, lambda i: pl.semaphore_signal(
            go.at[s], inc=1, device_id=frame_device(i), device_id_type=MESH))

    def ready_for_first():
        loop(0, 3, lambda m: pl.semaphore_signal(
            go_first, inc=1, device_id=unit_device(m), device_id_type=MESH))

    def send_out(s, lo, hi):
        loop(lo, hi, lambda i: send(
            dxs.at[s, i], l1o.at[s, u_m], s_o1.at[s], r_o1.at[s, u_m],
            frame_device(i)))

    def to_tokens(src, dst, ssem, rsem, first=0, frames=4):
        fr = pl.ds(first, frames)

        def rows(p):
            return src.at[fr, pl.ds(pl.multiple_of(p * 32, 32), 32), :]

        copy(rows(d), dst.at[d, fr], rsem)

        for p, to in peers():
            send(rows(p), dst.at[d, fr], ssem, rsem, to)

    def to_frames(src, dst, ssem, rsem, first):
        mine = pl.ds(pl.multiple_of(d * 32 + first, 16), 16)
        copy(src.at[d], dst.at[:, mine, :], rsem)

        for p, to in peers():
            send(src.at[p], dst.at[:, mine, :], ssem, rsem, to)

    def gain_row(s, l, j):
        return gn[s, l, u_h, j:j + 1, :]

    def spatial_fwd(s, frames=range(4)):
        gq, gk = gain_row(s, 0, 0), gain_row(s, 0, 1)
        b = s % 2
        for i in frames:
            ab = a_s[s, i]
            u = ab.astype(F32)
            (r,), (n,), (q,), (k,), (p,) = attend_fwd([u], gq, gk, None)
            pb = p.astype(BF)
            sp[b, i] = p
            spb[b, i] = pb
            sq[b, i] = q
            sk[b, i] = k
            sn[b, i] = n
            sr[b, i] = jnp.broadcast_to(r, n.shape)
            ys[s, i] = (u + dot(pb, ab, 0, 0)).astype(BF)

    def add_gains(s, l, dgq, dgk):
        gsum[s, 2 * l:2 * l + 1, :] += dgq
        gsum[s, 2 * l + 1:2 * l + 2, :] += dgk

    def spatial_bwd(s, first):
        gq, gk = gain_row(s, 0, 0), gain_row(s, 0, 1)
        b = s % 2
        two = (first, first + 1)
        dx, dgq, dgk = attend_bwd(
            [(dys[s, i], a_s[s, i], sp[b, i], spb[b, i], sq[b, i], sk[b, i], sn[b, i], sr[b, i])
             for i in two], gq, gk)
        for i, block in zip(two, dx):
            dxs[s, i] = block.astype(BF)
        add_gains(s, 0, dgq, dgk)

    ri = lax.broadcasted_iota(jnp.int32, (128, 128), 0)
    ci = lax.broadcasted_iota(jnp.int32, (128, 128), 1)
    same = (ri // 32) == (ci // 32)

    def by_token(src):
        xf[...] = src[...].reshape(FRAMES * 32, HD).astype(F32)

    def token_rows(b):
        return jnp.concatenate(
            [xf[pl.ds(b * 4 + t, FRAMES, stride=32), :] for t in range(4)], axis=0)

    def temporal_fwd(s):
        by_token(yt.at[s])
        gq, gk = gain_row(s, 1, 0), gain_row(s, 1, 1)
        for first in range(0, 8, 4):
            four = range(first, first + 4)
            us = [token_rows(b) for b in four]
            for b, u, r, n, q, k, p in zip(four, us, *attend_fwd(us, gq, gk, same)):
                tx[b] = u.astype(BF)
                tp[b] = p
                tpb[b] = p.astype(BF)
                tq[b] = q
                tk[b] = k
                tn[b] = n
                trr[b] = jnp.broadcast_to(r, n.shape)

    def temporal_bwd(s, first):
        gq, gk = gain_row(s, 1, 0), gain_row(s, 1, 1)
        four = range(first, first + 4)
        dx, dgq, dgk = attend_bwd(
            [(token_rows(b).astype(BF), tx[b], tp[b], tpb[b], tq[b], tk[b], tn[b], trr[b])
             for b in four], gq, gk)
        for b, block in zip(four, dx):
            for t in range(4):
                xo[pl.ds((b - first) * 4 + t, FRAMES, stride=16), :] = block[t * 32:(t + 1) * 32]
        add_gains(s, 1, dgq, dgk)
        dyt[s, first // 4] = xo[...].astype(BF).reshape(8, 4, 16, HD)

    def follow():
        @pl.when(jnp.logical_and(x != last, active))
        def _():
            hops_a()

    forward_a(last, follow)

    @pl.when(active)
    def _():
        wait(og_s, r_og)
        to_tokens(og_s, gt.at[last], s_g.at[last], r_g.at[last])
        wait(gn, r_gn)
        wait(a_s.at[last], r_a2.at[last])
        for part in range(2):
            spatial_fwd(last, range(2 * part, 2 * part + 2))
            to_tokens(ys.at[last], yt.at[last], s_y.at[last], r_y.at[last], 2 * part, 2)

        next_frames(last - 1)
        forward_a(last - 1)
        wait(yt.at[last], r_y.at[last])
        temporal_fwd(last)

        def section(step):
            s = last - step
            before = jnp.maximum(s - 1, 0)
            after = jnp.minimum(s + 1, last)
            wait(gt.at[s], r_g.at[s])
            by_token(gt.at[s])
            for part in range(2):
                temporal_bwd(s, 4 * part)
                to_frames(dyt.at[s, part], dys.at[s], s_dy.at[s], r_dy.at[s, part], 16 * part)

            @pl.when(s > 1)
            def _():
                next_frames(jnp.maximum(s - 2, 0))
                forward_a(jnp.maximum(s - 2, 0))

            @pl.when(s > 0)
            def _():
                wait(a_s.at[before], r_a2.at[before])
                spatial_fwd(before)
                to_tokens(ys.at[before], yt.at[before], s_y.at[before], r_y.at[before])

            @pl.when(s < last)
            def _():
                unit_gains(after)

            wait(dys.at[s, pl.ds(0, 2)], r_dy.at[s, 0])

            @pl.when(s == 0)
            def _():
                ready_for_first()

            wait(dys.at[s, pl.ds(2, 2)], r_dy.at[s, 1])
            spatial_bwd(s, 0)

            @pl.when(s > 0)
            def _():
                to_tokens(dxs.at[s], gt.at[before], s_g.at[before], r_g.at[before], 0, 2)

            spatial_bwd(s, 2)

            @pl.when(s > 0)
            def _():
                to_tokens(dxs.at[s], gt.at[before], s_g.at[before], r_g.at[before], 2, 2)
                wait(yt.at[before], r_y.at[before])
                temporal_fwd(before)

            share_gains(s)

            @pl.when(s > 0)
            def _():
                send_out(s, 0, 4)

        loop(0, SECTIONS, section)
        loop(0, last, lambda s: pl.semaphore_wait(go.at[s], 3))
        hop_out(3)
        hop_out(1)
        unit_gains(0)
        pl.semaphore_wait(go_first, 4)
        send_first(0, 4)
        hop_out(2)

    @pl.when(jnp.logical_not(active))
    def _():
        ready_for_first()
        wait(gn, r_gn)

        def next_section(j):
            pl.semaphore_wait(go.at[last - j], 3)
            forward_a(last - j)

        loop(1, SECTIONS, next_section)

        loop(0, SECTIONS - 1, lambda j: hop_out(last - j))

    wait(l1a.at[pl.ds(0, 3)], s_a1)
    wait(og_s.at[pl.ds(0, 3)], s_og)
    wait(gn.at[pl.ds(0, 3)], s_gn)

    loop(0, SECTIONS, lambda s: wait(l1a.at[s], s_a2.at[s]))

    @pl.when(active)
    def _():
        slots = gcol.reshape(32, 4, HD)

        def drain(s):
            wait(yt.at[s, pl.ds(0, 7)], s_y.at[s])
            wait(yt.at[s, pl.ds(0, 7)], s_g.at[s])
            wait(yt.at[s, pl.ds(0, 7)], s_dy.at[s])

            @pl.when(s > 0)
            def _():
                wait(dxs.at[s], s_o1.at[s])

            wait(gcol.at[s, pl.ds(0, 7)], s_p1.at[s])

            @pl.when(own & (s == x))
            def _():
                wait(slots.at[pl.ds(0, 15)], s_p2.at[s])

            @pl.when(jnp.logical_not(own & (s == x)))
            def _():
                wait(slots.at[pl.ds(0, 16)], s_p2.at[s])

        loop(0, SECTIONS, drain)

    wait(gains_ref, r_p2)
    wait(out_ref, r_o2)

    def drain(s):
        @pl.when(x != s)
        def _():
            wait(l1o.at[s], s_o2.at[s])

    loop(1, SECTIONS, drain)

    @pl.when(active)
    def _():
        wait(dxs.at[0], s_o1.at[0])


def hand_over(grads, gains, grads_out, gains_out, buf, gin, gbuf, s_in, s_out, s_g):
    first = [pltpu.make_async_copy(grads.at[m], buf.at[m], s_in.at[m]) for m in range(3)]
    second = [pltpu.make_async_copy(buf.at[m], grads_out.at[m], s_out.at[m]) for m in range(3)]
    arrive = pltpu.make_async_copy(gains, gin, s_g.at[0])
    leave = pltpu.make_async_copy(gbuf, gains_out, s_g.at[1])
    arrive.start()
    for one in first:
        one.start()
    arrive.wait()
    for row in range(4):
        for m in range(3):
            total = jnp.sum(gin[row, m], axis=0)
            for l in range(2):
                gbuf[l, row + 4 * m] = total[2 * l:2 * l + 2]
    leave.start()
    for one, other in zip(first, second):
        one.wait()
        other.start()
    leave.wait()
    for one in second:
        one.wait()


def per_device(section_inputs, out_grad, gains):
    def by_head(block):
        return block.reshape(TOKENS, HEADS, HD).transpose(1, 0, 2).reshape(3, 4, TOKENS, HD)

    a, og = by_head(section_inputs), by_head(out_grad)
    g = gains.reshape(2, 2, HEADS, HD).transpose(0, 2, 1, 3)
    V, D = pltpu.VMEM, pltpu.SemaphoreType.DMA
    s4, s43 = (SECTIONS,), (SECTIONS, 3)
    scratch = [
        V((4, 3, TOKENS, HD), BF),
        V((4, 4, TOKENS, HD), BF),
        V((4, TOKENS, HD), BF),
        V((4, 2, HEADS, 2, HD), F32),
        V((4, 4, TOKENS, HD), BF),
        V((4, 8, 4, 32, HD), BF),
        V((4, 8, 4, 32, HD), BF),
        V((4, 2, 8, 4, 16, HD), BF),
        V((4, 4, TOKENS, HD), BF),
        V((4, 4, TOKENS, HD), BF),
        V((4, 3, TOKENS, HD), BF),
        V((FRAMES * 32, HD), F32),
        V((FRAMES * 16, HD), F32),
        V((2, 4, TOKENS, TOKENS), F32),
        V((2, 4, TOKENS, TOKENS), BF),
        V((2, 4, TOKENS, HD), BF),
        V((2, 4, TOKENS, HD), BF),
        V((2, 4, TOKENS, HD), F32),
        V((2, 4, TOKENS, HD), F32),
        V((8, 128, HD), BF),
        V((8, 128, 128), F32),
        V((8, 128, 128), BF),
        V((8, 128, HD), BF),
        V((8, 128, HD), BF),
        V((8, 128, HD), F32),
        V((8, 128, HD), F32),
        V((4, 4, HD), F32),
        V((4, 8, 4, HD), F32),
        V((4, 4, HD), F32),
        D, D((SECTIONS, 6)), D(s4), D(s4), D, D, D, D, D(s4), D(s4), D(s4), D(s4), D(s4), D((SECTIONS, 2)),
        D(s4), D(s43), D(s4), D, D(s4), D(s4), D(s4), D, pltpu.SemaphoreType.REGULAR((3,)), pltpu.SemaphoreType.REGULAR,
    ]
    hbm = pl.BlockSpec(memory_space=pl.ANY)
    grads, gain_grads = pl.pallas_call(
        kernel,
        out_shape=(
            jax.ShapeDtypeStruct((3, 4, TOKENS, HD), BF),
            jax.ShapeDtypeStruct((4, 3, 4, 4, HD), F32),
        ),
        in_specs=[hbm, hbm, hbm],
        out_specs=(hbm, hbm),
        scratch_shapes=scratch,
        compiler_params=pltpu.CompilerParams(
            has_side_effects=True, collective_id=0, vmem_limit_bytes=60 * 1024 * 1024),
        name="sections_back",
    )(a, og, g)
    grads, gain_grads = pl.pallas_call(
        hand_over,
        out_shape=(
            jax.ShapeDtypeStruct(grads.shape, BF),
            jax.ShapeDtypeStruct((2, HEADS, 2, HD), F32),
        ),
        in_specs=[hbm, hbm],
        out_specs=(hbm, hbm),
        scratch_shapes=[V(grads.shape, BF), V(gain_grads.shape, F32),
                        V((2, HEADS, 2, HD), F32), D((3,)), D((3,)), D((2,))],
        compiler_params=pltpu.CompilerParams(vmem_limit_bytes=60 * 1024 * 1024),
        name="hand_over",
    )(grads, gain_grads)
    grads = grads.reshape(HEADS, TOKENS, HD).transpose(1, 0, 2).reshape(section_inputs.shape)
    return grads, gain_grads.transpose(0, 2, 1, 3)[None]


def solution(mesh):
    return jax.shard_map(
        per_device,
        mesh=mesh,
        in_specs=(
            P("pipe", "dp", "seq", None, None, None),
            P("dp", "seq", None, None, None),
            P("pipe", None, None, None, None),
        ),
        out_specs=(P("pipe", "dp", "seq", None, None, None), P("pipe", None, None, None, None)),
        check_vma=False,
    )
```
